32 devices in a mesh: groups: 2 (over y), seg: 4 (over z), space: 4 (over x, core).
Axes of the slice: x: 2, y: 2, z: 4, core: 2. Of those that a mesh axis runs over, the one named last changes fastest.
Arguments:
- basis: bfloat16 [8, 16, 3, 128, 256], P(('groups', 'seg'), 'space'), parts along dimension 0, may hold values from -6 to 6
- diffusivity: float32 [8, 16, 3, 128], P(('groups', 'seg'), 'space'), parts along dimension 0, may hold values from 0.05 to 0.15
- velocity: float32 [8, 3, 16, 3, 128], P(('groups', 'seg'), None, 'space'), parts along dimension 0, may hold values from -0.1 to 0.1
- step_counts: int32 [8], P(('groups', 'seg')), parts along dimension 0, may hold values from 2 to 4, as said below
- block_order: int32 [8, 16], P('groups'), parts along dimension 0, may hold values from 0 to 15, each once within a row
Outputs:
- image: bfloat16 [8, 16, 3, 128, 256], P(('groups', 'seg'), 'space'), parts along dimension 0
- monodromy: float32 [8, 256, 256], P(('groups', 'seg')), parts along dimension 0
The draws below stay inside these ranges and needn't reach their ends.
There are 2 independent parts, one for each index of `groups`. The reference program is written for one: setup_inputs(seed, part) draws one part's arguments, and reference() takes and returns one part's arrays. A program takes and returns all parts, laid end to end along the dimension named above; each array names one. Nothing has to cross between parts.
Inputs may be any that keep to these rules, and one draw needn't show every extreme that they name: `step_counts`: every segment takes two or more steps, and some segment takes 4. `block_order`: each row lists every block 0 to 15 once.
All inputs are finite; a program needn't handle non-finite values.
Results may differ from the reference program's by a relative error of at most 0.0052.
Values may be sent and summed in bfloat16 or wider, within the bound.
No kernel may reach another device: no remote copies, remote signals or barrier semaphores. Data moves between devices by JAX's collectives and lax.ppermute only.
A program may use at most 64 MiB of HBM per device.

```python
import math
import jax
import jax.numpy as jnp
from jax import lax

K = 256
BLOCK = 16
NB = 16
STEPS = 4
CY = 3
CZ = 128
SEG = 4
NX = 16


def draw_step_counts(key, part):
    first, second = jax.random.split(jax.random.fold_in(key, 17))
    counts = jax.random.randint(first, (SEG,), 2, STEPS + 1)
    chosen = jax.random.randint(second, (), 0, SEG)
    return jnp.where(jnp.arange(SEG) == chosen, STEPS, counts).astype(jnp.int32)


def shard_levels(key, shape, cuts, low, high):
    factor_of = 1.0
    for position, parts in cuts:
        steps = jax.random.uniform(jax.random.fold_in(jax.random.fold_in(key, 6), position), (parts,), jnp.float32, low / len(cuts), high / len(cuts))
        factor_of = factor_of * jnp.repeat(jnp.exp(steps), shape[position] // parts).reshape((-1,) + (1,) * (len(shape) - 1 - position))
    return factor_of


def normal_values(key, shape, deviation, most, shards=(), kind=jnp.bfloat16):
    level = shard_levels(key, shape, shards, -0.22, 0.18) if shards else 1.0
    array = jax.random.normal(key, shape, jnp.float32) * deviation * level
    return jnp.minimum(jnp.maximum(array, -most), most).astype(kind)


def setup_inputs(seed: int = 0, part: int = 0) -> dict:
    key_list = jax.random.split(jax.random.key(seed), 6)
    part_keys = jax.random.split(jax.random.fold_in(key_list[5], part), 6)
    return {
        "basis": normal_values(part_keys[0], (SEG, NX, CY, CZ, K), 1.0, 6.0, ((0, 4), (1, 4))),
        "diffusivity": jnp.clip(0.05 + 0.10000001 * jax.random.uniform(part_keys[1], (SEG, NX, CY, CZ), jnp.float32) ** shard_levels(part_keys[1], (SEG, NX, CY, CZ), ((0, 4), (1, 4)), -0.2, 0.2), 0.05, 0.15),
        "velocity": normal_values(part_keys[2], (SEG, 3, NX, CY, CZ), 0.04, 0.1, ((0, 4), (2, 4)), jnp.float32),
        "step_counts": draw_step_counts(jax.random.fold_in(jax.random.fold_in(key_list[5], part), 71), part),
        "block_order": jax.vmap(lambda own: jax.random.permutation(own, NB))(jax.random.split(part_keys[4], SEG)).reshape((SEG, NB)).astype(jnp.int32),
    }


coupling = 0.35

def step_once(window, diffusivity, velocity):
    wide = window.astype(jnp.float32)
    center = wide[1:-1]
    plus_x = wide[2:]
    minus_x = wide[:-2]
    plus_y = jnp.roll(center, -1, 1)
    minus_y = jnp.roll(center, 1, 1)
    plus_z = jnp.roll(center, -1, 2)
    minus_z = jnp.roll(center, 1, 2)
    spread = diffusivity[..., None]
    laplace = plus_x + minus_x + plus_y + minus_y + plus_z + minus_z - 6.0 * center
    drift = velocity[0][..., None] * (plus_x - minus_x) + velocity[1][..., None] * (plus_y - minus_y) + velocity[2][..., None] * (plus_z - minus_z)
    return (center + spread * laplace - 0.5 * drift).astype(jnp.bfloat16)

def block_perm(order):
    stored = jnp.arange(K, dtype=jnp.int32)
    which = stored // BLOCK
    onehot = which[:, None] == jnp.arange(order.shape[0], dtype=jnp.int32)[None, :]
    true_col = lax.optimization_barrier(jnp.sum(jnp.where(onehot, order[None, :], 0), axis=1)) * BLOCK + stored % BLOCK
    return (jnp.arange(K, dtype=jnp.int32)[:, None] == true_col[None, :]).astype(jnp.float32)

def propagator(raw_sums, left_order, right_order, cells):
    left = block_perm(left_order)
    right = block_perm(right_order)
    inner = jnp.dot(left, raw_sums, precision=lax.Precision.HIGHEST, preferred_element_type=jnp.float32)
    true_sums = jnp.dot(inner, right.T, precision=lax.Precision.HIGHEST, preferred_element_type=jnp.float32)
    return jnp.eye(K, dtype=jnp.float32) + coupling / math.sqrt(K * cells) * true_sums

def reference(basis, diffusivity, velocity, step_counts, block_order):
    following = jnp.roll(basis, -1, 0)
    next_order = jnp.roll(block_order, -1, 0)
    cells = NX * CY * CZ

    def segment(items):
        start, ahead, spread, drift, count, order_here, order_next = items
        state = start
        for turn in range(STEPS):
            window = jnp.pad(state, ((1, 1), (0, 0), (0, 0), (0, 0)))
            fresh = step_once(window, spread, drift)
            state = jnp.where(turn < count, fresh, state)
        raw_sums = lax.dot_general(ahead.reshape(-1, K), state.reshape(-1, K), (((0,), (0,)), ((), ())), preferred_element_type=jnp.float32)
        return (state, propagator(raw_sums, order_next, order_here, cells))
    image, props = lax.map(segment, (basis, following, diffusivity, velocity, step_counts, block_order, next_order))

    def advance(carry, prop):
        product = jnp.dot(prop, carry, precision=lax.Precision.HIGHEST, preferred_element_type=jnp.float32)
        return (product, product)
    _, monodromy = lax.scan(advance, jnp.eye(K, dtype=jnp.float32), props)
    return (image, monodromy)
```

```python
import math

import jax
import jax.numpy as jnp
from jax import lax
from jax.sharding import PartitionSpec as P

K = 256
BLOCK = 16
STEPS = 4
HALF = K // 2

coupling = 0.35


def swap(value, axis, bit):
    size = lax.axis_size(axis)
    return lax.ppermute(value, axis, [(i, i ^ bit) for i in range(size)])


def exchange_pairs(value, axis, first):
    size = lax.axis_size(axis)
    route = []
    for i in range(first, size - 1, 2):
        route += [(i, i + 1), (i + 1, i)]
    return lax.ppermute(value, axis, route)


def step_once(window, spread, drift):
    wide = window.astype(jnp.float32)
    center = wide[1:-1]
    plus_x = wide[2:]
    minus_x = wide[:-2]
    plus_y = jnp.roll(center, -1, 1)
    minus_y = jnp.roll(center, 1, 1)
    plus_z = jnp.roll(center, -1, 2)
    minus_z = jnp.roll(center, 1, 2)
    laplace = plus_x + minus_x + plus_y + minus_y + plus_z + minus_z - 6.0 * center
    change = (
        drift[0][..., None] * (plus_x - minus_x)
        + drift[1][..., None] * (plus_y - minus_y)
        + drift[2][..., None] * (plus_z - minus_z)
    )
    return (center + spread[..., None] * laplace - 0.5 * change).astype(jnp.bfloat16)


def block_perm(order):
    stored = jnp.arange(K, dtype=jnp.int32)
    which = stored // BLOCK
    onehot = which[:, None] == jnp.arange(order.shape[0], dtype=jnp.int32)[None, :]
    true_col = jnp.sum(jnp.where(onehot, order[None, :], 0), axis=1) * BLOCK + stored % BLOCK
    return (jnp.arange(K, dtype=jnp.int32)[:, None] == true_col[None, :]).astype(jnp.bfloat16)


def order_row(block_order, index):
    return lax.dynamic_slice_in_dim(block_order, index, 1, 0)[0]


def mul(left, right):
    return jnp.dot(left, right, preferred_element_type=jnp.float32)


def to_bf16(value):
    return value.astype(jnp.bfloat16)


def to_f32(value):
    return value.astype(jnp.float32)


def per_device(basis, diffusivity, velocity, step_counts, block_order):
    start = basis[0]
    layers = start.shape[0]
    width = STEPS
    here = lax.axis_index("seg")
    total = lax.axis_size("seg")
    place = lax.axis_index("space")
    slabs = lax.axis_size("space")
    core = place % 2
    cells = start.shape[0] * slabs * start.shape[1] * start.shape[2]
    count = step_counts[0]

    ahead = lax.ppermute(start, "seg", [((i + 1) % total, i) for i in range(total)])
    coefs = jnp.concatenate([diffusivity, velocity[0]], axis=0)
    far = exchange_pairs(start, "space", 1)
    near = exchange_pairs(start, "space", 0)
    far_coefs = exchange_pairs(coefs, "space", 1)
    near_coefs = exchange_pairs(coefs, "space", 0)
    even = core == 0
    before = jnp.where(even, far, near)[-width:]
    after = jnp.where(even, near, far)[:width]
    window = jnp.concatenate([before, start, after], axis=0)
    before_c = jnp.where(even, far_coefs, near_coefs)[:, -width:]
    after_c = jnp.where(even, near_coefs, far_coefs)[:, :width]
    coefs = jnp.concatenate([before_c, coefs, after_c], axis=1)
    for turn in range(STEPS):
        coefs = coefs[:, 1:-1]
        fresh = step_once(window, coefs[0], coefs[1:])
        window = jnp.where(turn < count, fresh, window[1:-1])
    state = window

    raw = lax.dot_general(
        ahead.reshape(-1, K),
        state.reshape(-1, K),
        (((0,), (0,)), ((), ())),
        preferred_element_type=jnp.float32,
    )
    left = block_perm(order_row(block_order, (here + 1) % total))
    right = block_perm(order_row(block_order, here))
    raw = to_bf16(mul(to_bf16(mul(left, to_bf16(raw))), right.T))
    low, high = raw[:, :HALF], raw[:, HALF:]
    mine = jnp.where(even, low, high)
    other = jnp.where(even, high, low)
    own = to_bf16(to_f32(mine) + to_f32(swap(other, "space", 1)))
    bit = 2
    summed = to_f32(own)
    while bit < slabs:
        summed = to_f32(to_bf16(summed))
        summed = summed + to_f32(swap(to_bf16(summed), "space", bit))
        bit *= 2
    half = to_bf16(summed * (coupling / math.sqrt(K * cells)))

    def whole(part):
        rest = swap(part, "space", 1)
        return jnp.where(
            even,
            jnp.concatenate([part, rest], axis=1),
            jnp.concatenate([rest, part], axis=1),
        )

    def my_half(full):
        return jnp.where(even, full[:, :HALF], full[:, HALF:])

    prefix = whole(half)
    block = prefix
    block_half = half
    bit = 1
    while bit < total:
        upper = (here // bit) % 2 == 1
        got = swap(block_half, "seg", bit)
        last = 2 * bit >= total
        if last:
            new = to_f32(my_half(prefix)) + to_f32(got) + mul(prefix, got)
            result = jnp.where(upper, new, to_f32(my_half(prefix)))
        else:
            got = whole(got)
            later = jnp.where(upper, block, got)
            earlier = jnp.where(upper, got, block)
            new = to_bf16(to_f32(later) + to_f32(earlier) + mul(later, earlier))
            extended = to_bf16(to_f32(prefix) + to_f32(got) + mul(prefix, got))
            prefix = jnp.where(upper, extended, prefix)
            block = new
            block_half = my_half(block)
        bit *= 2
    monodromy = whole(result) + jnp.eye(K, dtype=jnp.float32)
    return (state[None], monodromy[None])


def solution(mesh):
    in_specs = (
        P(("groups", "seg"), "space", None, None, None),
        P(("groups", "seg"), "space", None, None),
        P(("groups", "seg"), None, "space", None, None),
        P(("groups", "seg")),
        P("groups", None),
    )
    out_specs = (P(("groups", "seg"), "space", None, None, None), P(("groups", "seg"), None, None))
    return jax.shard_map(
        per_device, mesh=mesh, in_specs=in_specs, out_specs=out_specs, check_vma=False
    )
```

```python
import math

import jax
import jax.numpy as jnp
from jax import lax
from jax.experimental import pallas as pl
from jax.experimental.pallas import tpu as pltpu
from jax.sharding import PartitionSpec as P

K = 256
BLOCK = 16
STEPS = 4
HALF = K // 2

coupling = 0.35


def swap(value, axis, bit):
    size = lax.axis_size(axis)
    return lax.ppermute(value, axis, [(i, i ^ bit) for i in range(size)])


def exchange_pairs(value, axis, first):
    size = lax.axis_size(axis)
    route = []
    for i in range(first, size - 1, 2):
        route += [(i, i + 1), (i + 1, i)]
    return lax.ppermute(value, axis, route)


ROWS = 144
TOP = 8
CHUNK = 16
FIELDS = 4
NEAR_LAYERS = (6, 4, 2)


def spread_coefs(columns, column, flip, out, plane):
    def field(k):
        return jnp.broadcast_to(columns[:, column + k : column + k + 1], (columns.shape[0], HALF))

    diffusion = field(0)
    along_u = -field(1) if flip else field(1)
    along_y = field(2)
    along_z = field(3)
    out[plane, 0] = 1.0 - 6.0 * diffusion
    out[plane, 1] = diffusion - along_u
    out[plane, 2] = diffusion + along_u
    out[plane, 3] = diffusion - along_y
    out[plane, 4] = diffusion + along_y
    out[plane, 5] = diffusion - along_z
    out[plane, 6] = diffusion + along_z


def unpack_layer(source, index, dest, slot):
    ys, zs = source.shape[1], source.shape[2]
    for y in range(ys):
        for h in range(2):
            lanes = slice(h * HALF, (h + 1) * HALF)
            value = source[index, y, :, lanes].astype(jnp.float32)
            dest[slot, y, h, TOP : TOP + zs, :] = value
            dest[slot, y, h, TOP - 1 : TOP, :] = value[zs - 1 : zs]
            dest[slot, y, h, TOP + zs : TOP + zs + 1, :] = value[0:1]


def step_layer(source, index, coefs, layer, active, store):
    ys = source.shape[1]
    zs = coefs.shape[2]
    for y in range(ys):
        above, below = (y + 1) % ys, (y + ys - 1) % ys
        for z in range(0, zs, CHUNK):
            factor = [coefs[layer * ys + y, k, z : z + CHUNK, :] for k in range(7)]
            rows = slice(TOP + z, TOP + z + CHUNK)
            for h in range(2):
                center = source[index, y, h, rows, :]
                new = factor[0] * center
                new += factor[1] * source[index + 1, y, h, rows, :]
                new += factor[2] * source[index - 1, y, h, rows, :]
                new += factor[3] * source[index, above, h, rows, :]
                new += factor[4] * source[index, below, h, rows, :]
                new += factor[5] * source[index, y, h, TOP + z + 1 : TOP + z + CHUNK + 1, :]
                new += factor[6] * source[index, y, h, TOP + z - 1 : TOP + z + CHUNK - 1, :]
                if active is not None:
                    new = jnp.where(active, new, center)
                store(y, h, z, new.astype(jnp.bfloat16))


def into_level(dest, slot, zs):
    def store(y, h, z, rows):
        wide = rows.astype(jnp.float32)
        dest[slot, y, h, TOP + z : TOP + z + CHUNK, :] = wide
        if z == 0:
            dest[slot, y, h, TOP + zs : TOP + zs + 1, :] = wide[0:1]
        if z + CHUNK == zs:
            dest[slot, y, h, TOP - 1 : TOP, :] = wide[CHUNK - 1 : CHUNK]

    return store


def near_kernel(info, near, own, near_coefs, own_coefs, mid1, mid2, mid3, level0, level1, level2, level3, coefs):
    odd = info[0]
    count = info[1]
    ys, zs = own.shape[1], own.shape[2]
    group = ys * FIELDS
    table = jnp.concatenate(
        [own_coefs[...], near_coefs[...], jnp.zeros((128 - 2 * 4 * group, zs), jnp.float32)], axis=0
    ).T
    for j in range(6):
        u = j - 3
        for y in range(ys):
            if u < 0:
                spread_coefs(table, (4 + (-1 - u)) * group + y * FIELDS, True, coefs, j * ys + y)
            else:
                spread_coefs(table, u * group + y * FIELDS, False, coefs, j * ys + y)

    def fill(k, _):
        flipped = jnp.where(odd == 1, 3 - k, k)
        unpack_layer(near, flipped, level0, 3 - k)
        unpack_layer(own, 3 - flipped, level0, 4 + k)
        return 0

    lax.fori_loop(0, 4, fill, 0)
    levels = (level0, level1, level2, level3)
    for t, layers in enumerate(NEAR_LAYERS):
        source, dest = levels[t], levels[t + 1]
        active = None if t < 2 else count > t

        def one(j, _):
            step_layer(source, j + 1, coefs, j + t, active, into_level(dest, j, zs))
            return 0

        lax.fori_loop(0, layers, one, 0)
    mid1[...] = level1[4:6]
    mid2[...] = level2[2:4]
    mid3[...] = level3[...]


def far_kernel(info, own, far, own_coefs, far_coefs, mid1, mid2, mid3, out, level0, level1, level2, level3, coefs):
    odd = info[0]
    count = info[1]
    ys, zs = own.shape[1], own.shape[2]
    group = ys * FIELDS
    table = jnp.concatenate(
        [own_coefs[...], far_coefs[...], jnp.zeros((128 - 2 * 4 * group, zs), jnp.float32)], axis=0
    ).T
    for u in range(7):
        for y in range(ys):
            if u < 4:
                spread_coefs(table, u * group + y * FIELDS, False, coefs, u * ys + y)
            else:
                spread_coefs(table, (4 + 7 - u) * group + y * FIELDS, True, coefs, u * ys + y)

    def fill_own(k, _):
        unpack_layer(own, jnp.where(odd == 1, 2 + k, 1 - k), level0, k)
        return 0

    def fill_far(k, _):
        unpack_layer(far, jnp.where(odd == 1, k, 3 - k), level0, 2 + k)
        return 0

    lax.fori_loop(0, 2, fill_own, 0)
    lax.fori_loop(0, 4, fill_far, 0)
    level1[0:2] = mid1[...]
    level2[0:2] = mid2[...]
    level3[0:2] = mid3[...]
    levels = (level0, level1, level2, level3)
    for t in range(STEPS):
        source = levels[t]
        active = None if t < 2 else count > t

        def one(j, _):
            if t < STEPS - 1:
                store = into_level(levels[t + 1], 2 + j, zs)
            else:
                layer = jnp.where(odd == 1, j, 3 - j)

                def store(y, h, z, rows):
                    out[layer, y, z : z + CHUNK, h * HALF : (h + 1) * HALF] = rows

            step_layer(source, 1 + j, coefs, 3 - t + j, active, store)
            return 0

        lax.fori_loop(0, 4, one, 0)


def run_steps(info, near, own, far, near_coefs, own_coefs, far_coefs):
    ys, zs = own.shape[1], own.shape[2]
    vmem = pl.BlockSpec(memory_space=pltpu.VMEM)
    smem = pl.BlockSpec(memory_space=pltpu.SMEM)
    work = ys * zs * K

    def level(layers):
        return pltpu.VMEM((layers, ys, 2, ROWS, HALF), jnp.float32)

    def factors(layers):
        return pltpu.VMEM((layers * ys, 7, zs, HALF), jnp.float32)

    mid = jax.ShapeDtypeStruct((2, ys, 2, ROWS, HALF), jnp.float32)
    mids = pl.pallas_call(
        near_kernel,
        out_shape=(mid, mid, mid),
        in_specs=[smem] + [vmem] * 4,
        out_specs=(vmem,) * 3,
        scratch_shapes=[level(8), level(6), level(4), level(2), factors(6)],
        compiler_params=pltpu.CompilerParams(vmem_limit_bytes=36 * 2**20),
        cost_estimate=pl.CostEstimate(flops=12 * 20 * work, bytes_accessed=8 * 2**20, transcendentals=0),
    )(info, near, own, near_coefs, own_coefs)
    return pl.pallas_call(
        far_kernel,
        out_shape=jax.ShapeDtypeStruct(own.shape, own.dtype),
        in_specs=[smem] + [vmem] * 7,
        out_specs=vmem,
        scratch_shapes=[level(6)] * 4 + [factors(7)],
        compiler_params=pltpu.CompilerParams(vmem_limit_bytes=36 * 2**20),
        cost_estimate=pl.CostEstimate(flops=16 * 20 * work, bytes_accessed=8 * 2**20, transcendentals=0),
    )(info, own, far, own_coefs, far_coefs, *mids)


def block_perm(order):
    stored = jnp.arange(K, dtype=jnp.int32)
    which = stored // BLOCK
    onehot = which[:, None] == jnp.arange(order.shape[0], dtype=jnp.int32)[None, :]
    true_col = jnp.sum(jnp.where(onehot, order[None, :], 0), axis=1) * BLOCK + stored % BLOCK
    return (jnp.arange(K, dtype=jnp.int32)[:, None] == true_col[None, :]).astype(jnp.bfloat16)


def order_row(block_order, index):
    return lax.dynamic_slice_in_dim(block_order, index, 1, 0)[0]


def mul(left, right):
    return jnp.dot(left, right, preferred_element_type=jnp.float32)


def to_bf16(value):
    return value.astype(jnp.bfloat16)


def to_f32(value):
    return value.astype(jnp.float32)


def per_device(basis, diffusivity, velocity, step_counts, block_order):
    start = basis[0]
    here = lax.axis_index("seg")
    total = lax.axis_size("seg")
    place = lax.axis_index("space")
    slabs = lax.axis_size("space")
    core = place % 2
    cells = start.shape[0] * slabs * start.shape[1] * start.shape[2]
    count = step_counts[0]

    ahead = lax.ppermute(start, "seg", [((i + 1) % total, i) for i in range(total)])
    even = core == 0
    fields = jnp.concatenate([diffusivity, 0.5 * velocity[0]], axis=0)
    turned = fields[:, ::-1] * jnp.array([1.0, -1.0, 1.0, 1.0], jnp.float32)[:, None, None, None]
    coefs = jnp.where(even, turned, fields).transpose(1, 2, 0, 3).reshape(-1, fields.shape[-1])
    far = exchange_pairs(start, "space", 1)
    near = exchange_pairs(start, "space", 0)
    far_coefs = exchange_pairs(coefs, "space", 1)
    near_coefs = exchange_pairs(coefs, "space", 0)
    info = jnp.stack([core, count]).astype(jnp.int32)
    state = run_steps(info, near, start, far, near_coefs, coefs, far_coefs)

    raw = lax.dot_general(
        ahead.reshape(-1, K),
        state.reshape(-1, K),
        (((0,), (0,)), ((), ())),
        preferred_element_type=jnp.float32,
    )
    left = block_perm(order_row(block_order, (here + 1) % total))
    right = block_perm(order_row(block_order, here))
    raw = to_bf16(mul(to_bf16(mul(left, to_bf16(raw))), right.T))
    low, high = raw[:, :HALF], raw[:, HALF:]
    mine = jnp.where(even, low, high)
    other = jnp.where(even, high, low)
    own = to_bf16(to_f32(mine) + to_f32(swap(other, "space", 1)))
    bit = 2
    summed = to_f32(own)
    while bit < slabs:
        summed = to_f32(to_bf16(summed))
        summed = summed + to_f32(swap(to_bf16(summed), "space", bit))
        bit *= 2
    half = to_bf16(summed * (coupling / math.sqrt(K * cells)))

    def whole(part):
        rest = swap(part, "space", 1)
        return jnp.where(
            even,
            jnp.concatenate([part, rest], axis=1),
            jnp.concatenate([rest, part], axis=1),
        )

    def my_half(full):
        return jnp.where(even, full[:, :HALF], full[:, HALF:])

    prefix = whole(half)
    block = prefix
    block_half = half
    bit = 1
    while bit < total:
        upper = (here // bit) % 2 == 1
        got = swap(block_half, "seg", bit)
        last = 2 * bit >= total
        if last:
            new = to_f32(my_half(prefix)) + to_f32(got) + mul(prefix, got)
            result = jnp.where(upper, new, to_f32(my_half(prefix)))
        else:
            got = whole(got)
            later = jnp.where(upper, block, got)
            earlier = jnp.where(upper, got, block)
            new = to_bf16(to_f32(later) + to_f32(earlier) + mul(later, earlier))
            extended = to_bf16(to_f32(prefix) + to_f32(got) + mul(prefix, got))
            prefix = jnp.where(upper, extended, prefix)
            block = new
            block_half = my_half(block)
        bit *= 2
    monodromy = whole(result) + jnp.eye(K, dtype=jnp.float32)
    return (state[None], monodromy[None])


def solution(mesh):
    in_specs = (
        P(("groups", "seg"), "space", None, None, None),
        P(("groups", "seg"), "space", None, None),
        P(("groups", "seg"), None, "space", None, None),
        P(("groups", "seg")),
        P("groups", None),
    )
    out_specs = (P(("groups", "seg"), "space", None, None, None), P(("groups", "seg"), None, None))
    return jax.shard_map(
        per_device, mesh=mesh, in_specs=in_specs, out_specs=out_specs, check_vma=False
    )
```

```python
import functools
import math

import jax
import jax.numpy as jnp
from jax import lax
from jax.experimental import pallas as pl
from jax.experimental.pallas import tpu as pltpu
from jax.sharding import PartitionSpec as P

K = 256
BLOCK = 16
STEPS = 4
HALF = K // 2

coupling = 0.35


def swap(value, axis, bit):
    size = lax.axis_size(axis)
    return lax.ppermute(value, axis, [(i, i ^ bit) for i in range(size)])


def exchange_pairs(value, axis, first):
    size = lax.axis_size(axis)
    route = []
    for i in range(first, size - 1, 2):
        route += [(i, i + 1), (i + 1, i)]
    return lax.ppermute(value, axis, route)


ROWS = 144
TOP = 8
CHUNK = 16
FIELDS = 4
NEAR_LAYERS = (6, 4, 2)


def spread_coefs(columns, column, out, plane):
    def field(k):
        return jnp.broadcast_to(columns[:, column + k : column + k + 1], (columns.shape[0], HALF))

    diffusion = field(0)
    along_u = field(1)
    along_y = field(2)
    along_z = field(3)
    out[plane, 0] = 1.0 - 6.0 * diffusion
    out[plane, 1] = diffusion - along_u
    out[plane, 2] = diffusion + along_u
    out[plane, 3] = diffusion - along_y
    out[plane, 4] = diffusion + along_y
    out[plane, 5] = diffusion - along_z
    out[plane, 6] = diffusion + along_z


def coef_columns(fields, odd, backward, table):
    ys, layers, zs = fields.shape[1:]
    table[...] = jnp.zeros_like(table)
    sign = jnp.where(odd, 0.5, -0.5)
    for k in range(layers):
        flipped = layers - 1 - k
        x = jnp.where(odd, flipped, k) if backward else jnp.where(odd, k, flipped)
        for y in range(ys):
            for f in range(FIELDS):
                row = fields[f, y, pl.ds(x, 1), :]
                if f == 1:
                    row = row * sign
                elif f > 1:
                    row = row * 0.5
                at = (k * ys + y) * FIELDS + f
                table[at : at + 1, :] = row
    return table[...].T


def unpack_layer(source, index, dest, slot):
    ys, zs = source.shape[1], source.shape[2]
    for y in range(ys):
        for h in range(2):
            lanes = slice(h * HALF, (h + 1) * HALF)
            value = source[index, y, :, lanes].astype(jnp.float32)
            dest[slot, y, h, TOP : TOP + zs, :] = value
            dest[slot, y, h, TOP - 1 : TOP, :] = value[zs - 1 : zs]
            dest[slot, y, h, TOP + zs : TOP + zs + 1, :] = value[0:1]


def step_layer(source, index, coefs, layer, active, store):
    ys = source.shape[1]
    zs = coefs.shape[2]
    for z in range(0, zs, CHUNK):
        rows = slice(TOP + z, TOP + z + CHUNK)
        centers = [[source[index, y, h, rows, :] for h in range(2)] for y in range(ys)]
        for y in range(ys):
            factor = [coefs[layer * ys + y, k, z : z + CHUNK, :] for k in range(7)]
            for h in range(2):
                center = centers[y][h]
                new = factor[0] * center
                new += factor[1] * source[index + 1, y, h, rows, :]
                new += factor[2] * source[index - 1, y, h, rows, :]
                new += factor[3] * centers[(y + 1) % ys][h]
                new += factor[4] * centers[(y + ys - 1) % ys][h]
                new += factor[5] * source[index, y, h, TOP + z + 1 : TOP + z + CHUNK + 1, :]
                new += factor[6] * source[index, y, h, TOP + z - 1 : TOP + z + CHUNK - 1, :]
                if active is not None:
                    new = jnp.where(active, new, center)
                store(y, h, z, new.astype(jnp.bfloat16))


def into_level(dest, slot, zs):
    def store(y, h, z, rows):
        wide = rows.astype(jnp.float32)
        dest[slot, y, h, TOP + z : TOP + z + CHUNK, :] = wide
        if z == 0:
            dest[slot, y, h, TOP + zs : TOP + zs + 1, :] = wide[0:1]
        if z + CHUNK == zs:
            dest[slot, y, h, TOP - 1 : TOP, :] = wide[CHUNK - 1 : CHUNK]

    return store


def core_is_odd():
    return lax.axis_index("space") % 2 == 1


def near_kernel(
    counts, start, near, own_fields, near_fields, own_coefs, mid0, mid1, mid2, mid3,
    own, table, level0, level1, level2, level3, near_coefs, sem,
):
    odd = core_is_odd()
    fetch = pltpu.make_async_copy(start, own, sem)
    fetch.start()
    ys, zs = own.shape[1], own.shape[2]
    columns = coef_columns(own_fields, odd, False, table)
    for u in range(4):
        for y in range(ys):
            spread_coefs(columns, (u * ys + y) * FIELDS, own_coefs, u * ys + y)
    columns = coef_columns(near_fields, odd, True, table)
    for k in range(3):
        for y in range(ys):
            spread_coefs(columns, (k * ys + y) * FIELDS, near_coefs, (2 - k) * ys + y)

    def fill_near(k, _):
        unpack_layer(near, jnp.where(odd, 3 - k, k), level0, 3 - k)
        return 0

    def fill_own(k, _):
        unpack_layer(own, jnp.where(odd, k, 3 - k), level0, 4 + k)
        return 0

    lax.fori_loop(0, 4, fill_near, 0)
    fetch.wait()
    lax.fori_loop(0, 4, fill_own, 0)
    mid0[...] = level0[6:8]
    levels = (level0, level1, level2, level3)
    for t, layers in enumerate(NEAR_LAYERS):
        source, dest = levels[t], levels[t + 1]
        active = None if t < 2 else counts[0] > t
        half = layers // 2

        def near_one(j, _):
            step_layer(source, j + 1, near_coefs, j + t, active, into_level(dest, j, zs))
            return 0

        def own_one(j, _):
            step_layer(source, half + j + 1, own_coefs, j, active, into_level(dest, half + j, zs))
            return 0

        lax.fori_loop(0, half, near_one, 0)
        lax.fori_loop(0, half, own_one, 0)
    mid1[...] = level1[4:6]
    mid2[...] = level2[2:4]
    mid3[...] = level3[...]


def far_kernel(
    counts, far, far_fields, own_coefs, mid0, mid1, mid2, mid3,
    out, table, level0, level1, level2, level3, far_coefs,
):
    odd = core_is_odd()
    ys, zs = far.shape[1], far.shape[2]
    columns = coef_columns(far_fields, odd, True, table)
    for k in range(3):
        for y in range(ys):
            spread_coefs(columns, ((3 - k) * ys + y) * FIELDS, far_coefs, k * ys + y)

    def fill_far(k, _):
        unpack_layer(far, jnp.where(odd, k, 3 - k), level0, 2 + k)
        return 0

    lax.fori_loop(0, 4, fill_far, 0)
    level0[0:2] = mid0[...]
    level1[0:2] = mid1[...]
    level2[0:2] = mid2[...]
    level3[0:2] = mid3[...]
    levels = (level0, level1, level2, level3)
    for t in range(STEPS):
        source = levels[t]
        active = None if t < 2 else counts[0] > t

        def one(j, coefs, layer):
            if t < STEPS - 1:
                store = into_level(levels[t + 1], 2 + j, zs)
            else:
                place = jnp.where(odd, j, 3 - j)

                def store(y, h, z, rows):
                    out[place, y, z : z + CHUNK, h * HALF : (h + 1) * HALF] = rows

            step_layer(source, 1 + j, coefs, layer, active, store)

        def own_one(j, _):
            one(j, own_coefs, 3 - t + j)
            return 0

        def far_one(j, _):
            one(j, far_coefs, j - t - 1)
            return 0

        lax.fori_loop(0, t + 1, own_one, 0)
        if t < 3:
            lax.fori_loop(t + 1, 4, far_one, 0)


def mul(left, right):
    return jnp.dot(left, right, preferred_element_type=jnp.float32)


def to_bf16(value):
    return value.astype(jnp.bfloat16)


def to_f32(value):
    return value.astype(jnp.float32)


def product_kernel(order, ahead, state, image, out, rows, column_perm, sem):
    save = pltpu.make_async_copy(state, image, sem)
    save.start()
    here = lax.axis_index("seg")
    after = lax.rem(here + 1, lax.axis_size("seg"))
    blocks = K // BLOCK
    stored = lax.broadcasted_iota(jnp.int32, (BLOCK, K), 0)
    true = lax.broadcasted_iota(jnp.int32, (BLOCK, K), 1)
    for b in range(blocks):
        hit = (stored + order[here, b] * BLOCK) == true
        column_perm[b * BLOCK : (b + 1) * BLOCK, :] = jnp.where(hit, 1.0, 0.0).astype(jnp.bfloat16)
    left = ahead[...].reshape(-1, K)
    right = state[...].reshape(-1, K)
    raw = lax.dot_general(left, right, (((0,), (0,)), ((), ())), preferred_element_type=jnp.float32)
    raw = to_bf16(raw)
    for b in range(blocks):
        to = pl.multiple_of(order[after, b] * BLOCK, BLOCK)
        rows[pl.ds(to, BLOCK), :] = raw[b * BLOCK : (b + 1) * BLOCK]
    out[...] = to_bf16(mul(rows[...], column_perm[...]))
    save.wait()


def specs(kinds):
    spaces = {"s": pltpu.SMEM, "v": pltpu.VMEM, "a": pl.ANY}
    return [pl.BlockSpec(memory_space=spaces[kind]) for kind in kinds]


def params(megabytes):
    return pltpu.CompilerParams(vmem_limit_bytes=megabytes * 2**20)


def cost(flops, read):
    return pl.CostEstimate(flops=int(flops), bytes_accessed=int(read), transcendentals=0)


def near_steps(counts, start, near, own_fields, near_fields):
    ys, zs = start.shape[1], start.shape[2]

    def level(layers):
        return pltpu.VMEM((layers, ys, 2, ROWS, HALF), jnp.float32)

    mid = jax.ShapeDtypeStruct((2, ys, 2, ROWS, HALF), jnp.float32)
    return pl.pallas_call(
        near_kernel,
        out_shape=(jax.ShapeDtypeStruct((4 * ys, 7, zs, HALF), jnp.float32), mid, mid, mid, mid),
        in_specs=specs("savvv"),
        out_specs=tuple(specs("vvvvv")),
        scratch_shapes=[
            pltpu.VMEM(start.shape, start.dtype),
            pltpu.VMEM((128, zs), jnp.float32),
            level(8),
            level(6),
            level(4),
            level(2),
            pltpu.VMEM((3 * ys, 7, zs, HALF), jnp.float32),
            pltpu.SemaphoreType.DMA,
        ],
        compiler_params=params(36),
        cost_estimate=cost(0, 0),
    )(counts, start, near, own_fields, near_fields)


def far_steps(counts, far, far_fields, carried):
    ys, zs = far.shape[1], far.shape[2]
    level = pltpu.VMEM((6, ys, 2, ROWS, HALF), jnp.float32)
    return pl.pallas_call(
        far_kernel,
        out_shape=jax.ShapeDtypeStruct(far.shape, far.dtype),
        in_specs=specs("svvvvvvv"),
        out_specs=specs("v")[0],
        scratch_shapes=[pltpu.VMEM((128, zs), jnp.float32)]
        + [level] * 4
        + [pltpu.VMEM((3 * ys, 7, zs, HALF), jnp.float32)],
        compiler_params=params(36),
        cost_estimate=cost(0, 0),
    )(counts, far, far_fields, *carried)


def products(order, ahead, state):
    return pl.pallas_call(
        product_kernel,
        out_shape=(
            jax.ShapeDtypeStruct(state.shape, state.dtype),
            jax.ShapeDtypeStruct((K, K), jnp.bfloat16),
        ),
        in_specs=specs("svv"),
        out_specs=tuple(specs("av")),
        scratch_shapes=[
            pltpu.VMEM((K, K), jnp.bfloat16),
            pltpu.VMEM((K, K), jnp.bfloat16),
            pltpu.SemaphoreType.DMA,
        ],
        compiler_params=params(16),
        cost_estimate=cost(0, 0),
    )(order, ahead, state)


def merge_kernel(scale, straight, straight_other, diagonal, diagonal_other, own, tail, wide, block, half):
    odd = core_is_odd()
    upper = lax.axis_index("seg") % 2 == 1
    across = jnp.where(odd, straight_other[...], straight[...])
    along = jnp.where(odd, straight[...], straight_other[...])
    low = jnp.where(odd, diagonal_other[...], diagonal[...])
    high = jnp.where(odd, diagonal[...], diagonal_other[...])
    mine = (to_f32(own[...]) + to_f32(across)) * scale
    theirs = (to_f32(along) + to_f32(jnp.concatenate([low, high], axis=1))) * scale
    mine_low, theirs_low = to_bf16(mine), to_bf16(theirs)
    later = jnp.where(upper, mine_low, theirs_low)
    earlier = jnp.where(upper, theirs_low, mine_low)
    total = to_f32(mine_low) + to_f32(theirs_low) + mul(later, earlier)
    total_low = to_bf16(total)
    reach = jnp.where(upper, total, to_f32(mine_low))
    wide[...] = reach
    tail[...] = to_bf16(reach)
    block[...] = total_low
    half[...] = jnp.where(odd, total_low[:, HALF:], total_low[:, :HALF])


def merge(scale, straight, straight_other, diagonal, diagonal_other, own):
    full = jax.ShapeDtypeStruct((K, K), jnp.bfloat16)
    return pl.pallas_call(
        functools.partial(merge_kernel, scale),
        out_shape=(
            full,
            jax.ShapeDtypeStruct((K, K), jnp.float32),
            full,
            jax.ShapeDtypeStruct((K, HALF), jnp.bfloat16),
        ),
        in_specs=specs("vvvvv"),
        out_specs=tuple(specs("vvvv")),
        compiler_params=params(16),
        cost_estimate=cost(0, 0),
    )(straight, straight_other, diagonal, diagonal_other, own)


def last_kernel(bit, got, got_other, tail, wide, out):
    odd = core_is_odd()
    upper = lax.rem(lax.div(lax.axis_index("seg"), bit), 2) == 1
    low = jnp.where(odd, got_other[...], got[...])
    high = jnp.where(odd, got[...], got_other[...])
    before = jnp.concatenate([low, high], axis=1)
    more = to_f32(before) + mul(tail[...], before)
    row = lax.broadcasted_iota(jnp.int32, (K, K), 0)
    column = lax.broadcasted_iota(jnp.int32, (K, K), 1)
    reach = wide[...] + jnp.where(row == column, 1.0, 0.0)
    out[...] = jnp.where(upper, reach + more, reach)


def last(bit, got, got_other, tail, wide):
    return pl.pallas_call(
        functools.partial(last_kernel, bit),
        out_shape=jax.ShapeDtypeStruct((K, K), jnp.float32),
        in_specs=specs("vvvv"),
        out_specs=specs("v")[0],
        compiler_params=params(16),
        cost_estimate=cost(0, 0),
    )(got, got_other, tail, wide)


def mixed_swap(value, along, across, core_along):
    total, slabs = lax.axis_size("seg"), lax.axis_size("space")
    route = []
    for s in range(total):
        for x in range(slabs):
            if core_along:
                to = (s ^ along, x) if x % 2 else (s, x ^ across)
            else:
                to = (s ^ along, x ^ across)
            route.append((s * slabs + x, to[0] * slabs + to[1]))
    return lax.ppermute(value, ("seg", "space"), route)


def per_device(basis, diffusivity, velocity, step_counts, block_order):
    start = basis[0]
    total = lax.axis_size("seg")
    slabs = lax.axis_size("space")
    cells = start.shape[0] * slabs * start.shape[1] * start.shape[2]

    ahead = lax.ppermute(start, "seg", [((i + 1) % total, i) for i in range(total)])
    fields = jnp.concatenate([diffusivity, velocity[0]], axis=0).transpose(0, 2, 1, 3)
    far = exchange_pairs(start, "space", 1)
    near = exchange_pairs(start, "space", 0)
    far_fields = exchange_pairs(fields, "space", 1)
    near_fields = exchange_pairs(fields, "space", 0)
    carried = near_steps(step_counts, start, near, fields, near_fields)
    state = far_steps(step_counts, far, far_fields, carried)
    image, raw = products(block_order, ahead, state)

    bit = 1
    while 2 * bit < slabs:
        raw = to_bf16(to_f32(raw) + to_f32(swap(raw, "space", bit)))
        bit *= 2
    odd = lax.axis_index("space") % 2 == 1

    def my_half(full):
        return jnp.where(odd, full[:, HALF:], full[:, :HALF])

    straight = mixed_swap(raw, 1, bit, True)
    diagonal = mixed_swap(my_half(raw), 1, bit, False)
    straight_other = swap(straight, "space", 1)
    diagonal_other = swap(diagonal, "space", 1)
    scale = coupling / math.sqrt(K * cells)
    tail, wide, block, half = merge(scale, straight, straight_other, diagonal, diagonal_other, raw)

    bit = 2
    while 2 * bit < total:
        upper = (lax.axis_index("seg") // bit) % 2 == 1
        got = swap(half, "seg", bit)
        rest = swap(got, "space", 1)
        got = jnp.where(odd, jnp.concatenate([rest, got], 1), jnp.concatenate([got, rest], 1))
        later = jnp.where(upper, block, got)
        earlier = jnp.where(upper, got, block)
        wide = jnp.where(upper, wide + to_f32(got) + mul(tail, got), wide)
        tail = to_bf16(wide)
        block = to_bf16(to_f32(later) + to_f32(earlier) + mul(later, earlier))
        half = my_half(block)
        bit *= 2
    got = swap(half, "seg", bit)
    monodromy = last(bit, got, swap(got, "space", 1), tail, wide)
    return (image[None], monodromy[None])


def solution(mesh):
    in_specs = (
        P(("groups", "seg"), "space", None, None, None),
        P(("groups", "seg"), "space", None, None),
        P(("groups", "seg"), None, "space", None, None),
        P(("groups", "seg")),
        P("groups", None),
    )
    out_specs = (P(("groups", "seg"), "space", None, None, None), P(("groups", "seg"), None, None))
    return jax.shard_map(
        per_device, mesh=mesh, in_specs=in_specs, out_specs=out_specs, check_vma=False
    )
```

```python
import math

import jax
import jax.numpy as jnp
from jax import lax
from jax.experimental import pallas as pl
from jax.experimental.pallas import tpu as pltpu
from jax.sharding import PartitionSpec as P

K = 256
BLOCK = 16
STEPS = 4
HALF = K // 2

coupling = 0.35


def swap(value, axis, bit):
    size = lax.axis_size(axis)
    return lax.ppermute(value, axis, [(i, i ^ bit) for i in range(size)])


def exchange_pairs(value, axis, first):
    size = lax.axis_size(axis)
    route = []
    for i in range(first, size - 1, 2):
        route += [(i, i + 1), (i + 1, i)]
    return lax.ppermute(value, axis, route)


ROWS = 144
TOP = 8
CHUNK = 16
FIELDS = 4
NEAR_LAYERS = (6, 4, 2)


def spread_coefs(columns, column, out, plane):
    def field(k):
        return jnp.broadcast_to(columns[:, column + k : column + k + 1], (columns.shape[0], HALF))

    diffusion = field(0)
    along_u = field(1)
    along_y = field(2)
    along_z = field(3)
    out[plane, 0] = 1.0 - 6.0 * diffusion
    out[plane, 1] = diffusion - along_u
    out[plane, 2] = diffusion + along_u
    out[plane, 3] = diffusion - along_y
    out[plane, 4] = diffusion + along_y
    out[plane, 5] = diffusion - along_z
    out[plane, 6] = diffusion + along_z


def coef_columns(fields, odd, backward, table):
    ys, layers, zs = fields.shape[1:]
    table[...] = jnp.zeros_like(table)
    sign = jnp.where(odd, 0.5, -0.5)
    for k in range(layers):
        flipped = layers - 1 - k
        x = jnp.where(odd, flipped, k) if backward else jnp.where(odd, k, flipped)
        for y in range(ys):
            for f in range(FIELDS):
                row = fields[f, y, pl.ds(x, 1), :]
                if f == 1:
                    row = row * sign
                elif f > 1:
                    row = row * 0.5
                at = (k * ys + y) * FIELDS + f
                table[at : at + 1, :] = row
    return table[...].T


def unpack_layer(source, index, dest, slot):
    ys, zs = source.shape[1], source.shape[2]
    for y in range(ys):
        for h in range(2):
            lanes = slice(h * HALF, (h + 1) * HALF)
            value = source[index, y, :, lanes].astype(jnp.float32)
            dest[slot, y, h, TOP : TOP + zs, :] = value
            dest[slot, y, h, TOP - 1 : TOP, :] = value[zs - 1 : zs]
            dest[slot, y, h, TOP + zs : TOP + zs + 1, :] = value[0:1]


def step_layer(minus, here, plus, coefs, layer, active, store):
    level, slot = here
    ys = level.shape[1]
    zs = coefs.shape[2]
    for z in range(0, zs, CHUNK):
        rows = slice(TOP + z, TOP + z + CHUNK)
        centers = [[level[slot, y, h, rows, :] for h in range(2)] for y in range(ys)]
        for y in range(ys):
            factor = [coefs[layer * ys + y, k, z : z + CHUNK, :] for k in range(7)]
            for h in range(2):
                center = centers[y][h]
                new = factor[0] * center
                new += factor[1] * plus[0][plus[1], y, h, rows, :]
                new += factor[2] * minus[0][minus[1], y, h, rows, :]
                new += factor[3] * centers[(y + 1) % ys][h]
                new += factor[4] * centers[(y + ys - 1) % ys][h]
                new += factor[5] * level[slot, y, h, TOP + z + 1 : TOP + z + CHUNK + 1, :]
                new += factor[6] * level[slot, y, h, TOP + z - 1 : TOP + z + CHUNK - 1, :]
                if active is not None:
                    new = jnp.where(active, new, center)
                store(y, h, z, new.astype(jnp.bfloat16))


def into_level(dest, slot, zs):
    def store(y, h, z, rows):
        wide = rows.astype(jnp.float32)
        dest[slot, y, h, TOP + z : TOP + z + CHUNK, :] = wide
        if z == 0:
            dest[slot, y, h, TOP + zs : TOP + zs + 1, :] = wide[0:1]
        if z + CHUNK == zs:
            dest[slot, y, h, TOP - 1 : TOP, :] = wide[CHUNK - 1 : CHUNK]

    return store


def core_is_odd():
    return lax.axis_index("space") % 2 == 1


def coefs_kernel(
    own_fields, near_fields, start, order_home, own_coefs, near_coefs, order_here, order_next, own,
    table, order, columns, sems,
):
    fetch = pltpu.make_async_copy(start, own, sems.at[0])
    fetch_order = pltpu.make_async_copy(order_home, order, sems.at[1])
    fetch_order.start()
    fetch.start()
    odd = core_is_odd()
    ys = own_fields.shape[1]
    turned = coef_columns(own_fields, odd, False, table)
    for u in range(4):
        for y in range(ys):
            spread_coefs(turned, (u * ys + y) * FIELDS, own_coefs, u * ys + y)
    turned = coef_columns(near_fields, odd, True, table)
    for k in range(3):
        for y in range(ys):
            spread_coefs(turned, (k * ys + y) * FIELDS, near_coefs, (2 - k) * ys + y)

    fetch_order.wait()
    segments, blocks = order.shape
    block = lax.broadcasted_iota(jnp.int32, (blocks, K), 0)
    stored = lax.broadcasted_iota(jnp.int32, (blocks, K), 1)
    inside = jnp.where(lax.div(stored, BLOCK) == block, float(BLOCK), 0.0).astype(jnp.bfloat16)
    first = mul(order[...].astype(jnp.float32).astype(jnp.bfloat16), inside)
    offset = lax.rem(lax.broadcasted_iota(jnp.int32, first.shape, 1), BLOCK)
    columns[...] = first.astype(jnp.int32) + offset
    here = lax.axis_index("seg")
    after = lax.rem(here + 1, lax.axis_size("seg"))
    row = lax.broadcasted_iota(jnp.int32, (K, K), 0)
    for segment, out in ((here, order_here), (after, order_next)):
        out[...] = jnp.where(row == columns[pl.ds(segment, 1), :], 1.0, 0.0).astype(jnp.bfloat16)
    fetch.wait()


def near_kernel(counts, own, near, own_coefs, near_coefs, level0, level1, level2, level3):
    odd = core_is_odd()
    zs = own.shape[2]

    def fill(k, _):
        unpack_layer(near, jnp.where(odd, 3 - k, k), level0, 3 - k)
        unpack_layer(own, jnp.where(odd, k, 3 - k), level0, 4 + k)
        return 0

    lax.fori_loop(0, 4, fill, 0)
    levels = (level0, level1, level2, level3)
    for t, layers in enumerate(NEAR_LAYERS):
        source, dest = levels[t], levels[t + 1]
        active = None if t < 2 else counts[0] > t
        half = layers // 2

        def one(j, coefs, layer):
            refs = [(source, j + k) for k in range(3)]
            step_layer(*refs, coefs, layer, active, into_level(dest, j, zs))

        def near_one(j, _):
            one(j, near_coefs, j + t)
            return 0

        def own_one(j, _):
            one(half + j, own_coefs, j)
            return 0

        lax.fori_loop(0, half, near_one, 0)
        lax.fori_loop(0, half, own_one, 0)


def far_kernel(
    counts, far, far_fields, own_coefs, near0, near1, near2, near3,
    out, table, level0, level1, level2, level3, far_coefs,
):
    odd = core_is_odd()
    ys, zs = far.shape[1], far.shape[2]
    columns = coef_columns(far_fields, odd, True, table)
    for k in range(3):
        for y in range(ys):
            spread_coefs(columns, ((3 - k) * ys + y) * FIELDS, far_coefs, k * ys + y)

    def fill_far(k, _):
        unpack_layer(far, jnp.where(odd, k, 3 - k), level0, k)
        return 0

    lax.fori_loop(0, 4, fill_far, 0)
    nears = (near0, near1, near2, near3)
    levels = (level0, level1, level2, level3)
    for t in range(STEPS):
        near, source = nears[t], levels[t]
        end = near.shape[0]
        active = None if t < 2 else counts[0] > t

        def one(j, refs, is_far):
            if t < STEPS - 1:
                store = into_level(levels[t + 1], j, zs)
            else:
                place = jnp.where(odd, j, 3 - j)

                def store(y, h, z, rows):
                    out[place, y, z : z + CHUNK, h * HALF : (h + 1) * HALF] = rows

            if is_far:
                step_layer(*refs, far_coefs, j - t - 1, active, store)
            else:
                step_layer(*refs, own_coefs, 3 - t + j, active, store)

        one(0, ((near, end - 2), (near, end - 1), (source, 0)), False)
        one(1, ((near, end - 1), (source, 0), (source, 1)), t < 1)

        def own_one(j, _):
            one(j, [(source, j - 2 + k) for k in range(3)], False)
            return 0

        def far_one(j, _):
            one(j, [(source, j - 2 + k) for k in range(3)], True)
            return 0

        split = max(t + 1, 2)
        if split > 2:
            lax.fori_loop(2, split, own_one, 0)
        if split < 4:
            lax.fori_loop(split, 4, far_one, 0)


def mul(left, right):
    return jnp.dot(left, right, preferred_element_type=jnp.float32)


def to_bf16(value):
    return value.astype(jnp.bfloat16)


def to_f32(value):
    return value.astype(jnp.float32)


def product_kernel(ahead, state, order_next, order_here, image, out, sem):
    save = pltpu.make_async_copy(state, image, sem)
    save.start()
    left = ahead[...].reshape(-1, K)
    right = state[...].reshape(-1, K)
    raw = lax.dot_general(left, right, (((0,), (0,)), ((), ())), preferred_element_type=jnp.float32)
    raw = to_bf16(mul(order_next[...], to_bf16(raw)))
    turned = (((1,), (1,)), ((), ()))
    out[...] = to_bf16(lax.dot_general(raw, order_here[...], turned, preferred_element_type=jnp.float32))
    save.wait()


def specs(kinds):
    spaces = {"s": pltpu.SMEM, "v": pltpu.VMEM, "a": pl.ANY, "h": pltpu.HBM}
    return [pl.BlockSpec(memory_space=spaces[kind]) for kind in kinds]


def params(megabytes):
    return pltpu.CompilerParams(vmem_limit_bytes=megabytes * 2**20)


def cost(flops, read):
    return pl.CostEstimate(flops=int(flops), bytes_accessed=int(read), transcendentals=0)


def pinned(value):
    return pltpu.with_memory_space_constraint(value, pltpu.HBM)


def spread(fields, near_fields, start, order):
    zs = fields.shape[3]
    ys = fields.shape[1]

    def factors(layers):
        return jax.ShapeDtypeStruct((layers * ys, 7, zs, HALF), jnp.float32)

    perm = jax.ShapeDtypeStruct((K, K), jnp.bfloat16)
    return pl.pallas_call(
        coefs_kernel,
        out_shape=(factors(4), factors(3), perm, perm, jax.ShapeDtypeStruct(start.shape, start.dtype)),
        in_specs=specs("vvhh"),
        out_specs=tuple(specs("vvvvv")),
        scratch_shapes=[
            pltpu.VMEM((128, zs), jnp.float32),
            pltpu.VMEM(order.shape, jnp.int32),
            pltpu.VMEM((order.shape[0], K), jnp.int32),
            pltpu.SemaphoreType.DMA((2,)),
        ],
        compiler_params=params(8),
        cost_estimate=cost(0, 6 * 2**20),
    )(fields, near_fields, pinned(start), pinned(order))


def near_steps(counts, start, near, own_coefs, near_coefs):
    ys = start.shape[1]
    return pl.pallas_call(
        near_kernel,
        out_shape=tuple(
            jax.ShapeDtypeStruct((layers, ys, 2, ROWS, HALF), jnp.float32) for layers in (8, *NEAR_LAYERS)
        ),
        in_specs=specs("svvvv"),
        out_specs=tuple(specs("vvvv")),
        compiler_params=params(8),
        cost_estimate=cost(0, 0),
    )(counts, start, near, own_coefs, near_coefs)


def far_steps(counts, far, far_fields, own_coefs, levels):
    ys, zs = far.shape[1], far.shape[2]
    level = pltpu.VMEM((4, ys, 2, ROWS, HALF), jnp.float32)
    return pl.pallas_call(
        far_kernel,
        out_shape=jax.ShapeDtypeStruct(far.shape, far.dtype),
        in_specs=specs("svvvvvvv"),
        out_specs=specs("v")[0],
        scratch_shapes=[pltpu.VMEM((128, zs), jnp.float32)]
        + [level] * 4
        + [pltpu.VMEM((3 * ys, 7, zs, HALF), jnp.float32)],
        compiler_params=params(24),
        cost_estimate=cost(0, 0),
    )(counts, far, far_fields, own_coefs, *levels)


def products(ahead, state, order_next, order_here):
    return pl.pallas_call(
        product_kernel,
        out_shape=(
            jax.ShapeDtypeStruct(state.shape, state.dtype),
            jax.ShapeDtypeStruct((K, K), jnp.bfloat16),
        ),
        in_specs=specs("vvvv"),
        out_specs=tuple(specs("av")),
        scratch_shapes=[pltpu.SemaphoreType.DMA],
        compiler_params=params(16),
        cost_estimate=cost(0, 0),
    )(ahead, state, order_next, order_here)


def mixed_swap(value, along, across, core_along):
    total, slabs = lax.axis_size("seg"), lax.axis_size("space")
    route = []
    for s in range(total):
        for x in range(slabs):
            if core_along:
                to = (s ^ along, x) if x % 2 else (s, x ^ across)
            else:
                to = (s ^ along, x ^ across)
            route.append((s * slabs + x, to[0] * slabs + to[1]))
    return lax.ppermute(value, ("seg", "space"), route)


def per_device(basis, diffusivity, velocity, step_counts, block_order):
    start = basis[0]
    total = lax.axis_size("seg")
    slabs = lax.axis_size("space")
    cells = start.shape[0] * slabs * start.shape[1] * start.shape[2]

    ahead = lax.ppermute(start, "seg", [((i + 1) % total, i) for i in range(total)])
    fields = jnp.concatenate([diffusivity, velocity[0]], axis=0).transpose(0, 2, 1, 3)
    far = exchange_pairs(start, "space", 1)
    near = exchange_pairs(start, "space", 0)
    far_fields = exchange_pairs(fields, "space", 1)
    near_fields = exchange_pairs(fields, "space", 0)
    own_coefs, near_coefs, order_here, order_next, own = spread(fields, near_fields, start, block_order)
    levels = near_steps(step_counts, own, near, own_coefs, near_coefs)
    state = far_steps(step_counts, far, far_fields, own_coefs, levels)
    image, raw = products(ahead, state, order_next, order_here)

    bit = 1
    while 2 * bit < slabs:
        raw = to_bf16(to_f32(raw) + to_f32(swap(raw, "space", bit)))
        bit *= 2
    odd = lax.axis_index("space") % 2 == 1

    def my_half(full):
        return jnp.where(odd, full[:, HALF:], full[:, :HALF])

    def both_halves(part):
        rest = swap(part, "space", 1)
        return jnp.where(odd, jnp.concatenate([rest, part], 1), jnp.concatenate([part, rest], 1))

    straight = mixed_swap(raw, 1, bit, True)
    diagonal = mixed_swap(my_half(raw), 1, bit, False)
    straight_other = swap(straight, "space", 1)
    diagonal_other = swap(diagonal, "space", 1)
    scale = coupling / math.sqrt(K * cells)
    across = jnp.where(odd, straight_other, straight)
    along = jnp.where(odd, straight, straight_other)
    diagonal = jnp.where(odd, jnp.concatenate([diagonal_other, diagonal], 1), jnp.concatenate([diagonal, diagonal_other], 1))
    mine = to_bf16((to_f32(raw) + to_f32(across)) * scale)
    theirs = to_bf16((to_f32(along) + to_f32(diagonal)) * scale)
    def chained(later, earlier):
        return to_f32(later) + to_f32(earlier) + mul(later, earlier)

    upper = lax.axis_index("seg") % 2 == 1
    later = jnp.where(upper, mine, theirs)
    earlier = jnp.where(upper, theirs, mine)
    half = to_bf16(to_f32(my_half(later)) + to_f32(my_half(earlier)) + mul(later, my_half(earlier)))
    block = chained(later, earlier)
    wide = jnp.where(upper, block, to_f32(mine))
    bit = 2
    while bit < total:
        upper = (lax.axis_index("seg") // bit) % 2 == 1
        got = both_halves(swap(half, "seg", bit))
        wide = jnp.where(upper, wide + to_f32(got) + mul(to_bf16(wide), got), wide)
        block = to_bf16(block)
        later = jnp.where(upper, block, got)
        earlier = jnp.where(upper, got, block)
        block = chained(later, earlier)
        half = to_bf16(my_half(block))
        bit *= 2
    monodromy = wide + jnp.eye(K, dtype=jnp.float32)
    return (image[None], monodromy[None])


def solution(mesh):
    in_specs = (
        P(("groups", "seg"), "space", None, None, None),
        P(("groups", "seg"), "space", None, None),
        P(("groups", "seg"), None, "space", None, None),
        P(("groups", "seg")),
        P("groups", None),
    )
    out_specs = (P(("groups", "seg"), "space", None, None, None), P(("groups", "seg"), None, None))
    return jax.shard_map(
        per_device, mesh=mesh, in_specs=in_specs, out_specs=out_specs, check_vma=False
    )
```

```python
import math

import jax
import jax.numpy as jnp
from jax import lax
from jax.experimental import pallas as pl
from jax.experimental.pallas import tpu as pltpu
from jax.sharding import PartitionSpec as P

K = 256
BLOCK = 16
STEPS = 4
HALF = K // 2

coupling = 0.35


def swap(value, axis, bit):
    size = lax.axis_size(axis)
    return lax.ppermute(value, axis, [(i, i ^ bit) for i in range(size)])


def exchange_pairs(value, axis, first):
    size = lax.axis_size(axis)
    route = []
    for i in range(first, size - 1, 2):
        route += [(i, i + 1), (i + 1, i)]
    return lax.ppermute(value, axis, route)


ROWS = 144
TOP = 8
CHUNK = 16
FIELDS = 4
NEAR_LAYERS = (6, 4, 2)


def spread_coefs(columns, column, out, plane):
    def field(k):
        return jnp.broadcast_to(columns[:, column + k : column + k + 1], (columns.shape[0], HALF))

    diffusion = field(0)
    along_u = field(1)
    along_y = field(2)
    along_z = field(3)
    out[plane, 0] = 1.0 - 6.0 * diffusion
    out[plane, 1] = diffusion - along_u
    out[plane, 2] = diffusion + along_u
    out[plane, 3] = diffusion - along_y
    out[plane, 4] = diffusion + along_y
    out[plane, 5] = diffusion - along_z
    out[plane, 6] = diffusion + along_z


def coef_columns(fields, ys, odd, backward, table):
    layers = fields.shape[0] // (ys * FIELDS)
    table[...] = jnp.zeros_like(table)
    sign = jnp.where(odd, 0.5, -0.5)
    for k in range(layers):
        flipped = layers - 1 - k
        x = jnp.where(odd, flipped, k) if backward else jnp.where(odd, k, flipped)
        for y in range(ys):
            for f in range(FIELDS):
                row = fields[pl.ds((f * ys + y) * layers + x, 1), :]
                if f == 1:
                    row = row * sign
                elif f > 1:
                    row = row * 0.5
                at = (k * ys + y) * FIELDS + f
                table[at : at + 1, :] = row
    return table[...].T


def unpack_layer(source, index, ys, dest, slot):
    zs = source.shape[1]
    for y in range(ys):
        for h in range(2):
            value = source[index * ys + y, :, h * HALF : (h + 1) * HALF].astype(jnp.float32)
            dest[slot, y, h, TOP : TOP + zs, :] = value
            dest[slot, y, h, TOP - 1 : TOP, :] = value[zs - 1 : zs]
            dest[slot, y, h, TOP + zs : TOP + zs + 1, :] = value[0:1]


def step_layer(minus, here, plus, coefs, layer, active, store):
    level, slot = here
    ys = level.shape[1]
    zs = coefs.shape[2]
    for z in range(0, zs, CHUNK):
        rows = slice(TOP + z, TOP + z + CHUNK)
        centers = [[level[slot, y, h, rows, :] for h in range(2)] for y in range(ys)]
        for y in range(ys):
            factor = [coefs[layer * ys + y, k, z : z + CHUNK, :] for k in range(7)]
            for h in range(2):
                center = centers[y][h]
                new = factor[0] * center
                new += factor[1] * plus[0][plus[1], y, h, rows, :]
                new += factor[2] * minus[0][minus[1], y, h, rows, :]
                new += factor[3] * centers[(y + 1) % ys][h]
                new += factor[4] * centers[(y + ys - 1) % ys][h]
                new += factor[5] * level[slot, y, h, TOP + z + 1 : TOP + z + CHUNK + 1, :]
                new += factor[6] * level[slot, y, h, TOP + z - 1 : TOP + z + CHUNK - 1, :]
                if active is not None:
                    new = jnp.where(active, new, center)
                store(y, h, z, new.astype(jnp.bfloat16))


def into_level(dest, slot, zs):
    def store(y, h, z, rows):
        wide = rows.astype(jnp.float32)
        dest[slot, y, h, TOP + z : TOP + z + CHUNK, :] = wide
        if z == 0:
            dest[slot, y, h, TOP + zs : TOP + zs + 1, :] = wide[0:1]
        if z + CHUNK == zs:
            dest[slot, y, h, TOP - 1 : TOP, :] = wide[CHUNK - 1 : CHUNK]

    return store


def core_is_odd():
    return lax.axis_index("space") % 2 == 1


def pack_kernel(start, diffusivity, velocity, first, second, fields, spread_home, drift_home, sems):
    odd = core_is_odd()
    half = second.shape[0]
    here = jnp.where(odd, half, 0)
    there = jnp.where(odd, 0, half)
    small = (
        pltpu.make_async_copy(diffusivity, spread_home, sems.at[0]),
        pltpu.make_async_copy(velocity, drift_home, sems.at[1]),
    )
    copies = (
        pltpu.make_async_copy(start.at[pl.ds(here, half)], first.at[pl.ds(0, half)], sems.at[2]),
        pltpu.make_async_copy(start.at[pl.ds(there, half)], second, sems.at[3]),
    )
    for copy in small + copies:
        copy.start()
    for copy in small:
        copy.wait()
    ys, layers = spread_home.shape[0], spread_home.shape[1]
    for y in range(ys):
        for f in range(FIELDS):
            at = (f * ys + y) * layers
            fields[at : at + layers, :] = spread_home[y] if f == 0 else drift_home[f - 1, y]
    value = fields[...]
    high = to_bf16(value)
    rest = value - to_f32(high)
    middle = to_bf16(rest)
    low = to_bf16(rest - to_f32(middle))
    rows = value.shape[0]
    first[half, :rows, :HALF] = high
    first[half, :rows, HALF:] = middle
    first[half, rows : 2 * rows, :HALF] = low
    first[half, rows : 2 * rows, HALF:] = jnp.zeros_like(low)
    if first.shape[1] > 2 * rows:
        first[half, 2 * rows :, :] = jnp.zeros((first.shape[1] - 2 * rows, K), jnp.bfloat16)
    for copy in copies:
        copy.wait()


def unpack_fields(packed, fields):
    rows = fields.shape[0]
    at = packed.shape[0] - 1
    high = to_f32(packed[at, :rows, :HALF])
    middle = to_f32(packed[at, :rows, HALF:])
    low = to_f32(packed[at, rows : 2 * rows, :HALF])
    fields[...] = high + (middle + low)


def coefs_kernel(
    own_fields, near_first, order_home, own_coefs, near_coefs, order_here, order_next,
    near_fields, table, order, columns, sem,
):
    fetch = pltpu.make_async_copy(order_home, order, sem)
    fetch.start()
    odd = core_is_odd()
    ys = own_coefs.shape[0] // 4
    unpack_fields(near_first, near_fields)
    turned = coef_columns(own_fields, ys, odd, False, table)
    for u in range(4):
        for y in range(ys):
            spread_coefs(turned, (u * ys + y) * FIELDS, own_coefs, u * ys + y)
    turned = coef_columns(near_fields, ys, odd, True, table)
    for k in range(3):
        for y in range(ys):
            spread_coefs(turned, (k * ys + y) * FIELDS, near_coefs, (2 - k) * ys + y)

    fetch.wait()
    segments, blocks = order.shape
    block = lax.broadcasted_iota(jnp.int32, (blocks, K), 0)
    stored = lax.broadcasted_iota(jnp.int32, (blocks, K), 1)
    inside = jnp.where(lax.div(stored, BLOCK) == block, float(BLOCK), 0.0).astype(jnp.bfloat16)
    first = mul(order[...].astype(jnp.float32).astype(jnp.bfloat16), inside)
    offset = lax.rem(lax.broadcasted_iota(jnp.int32, first.shape, 1), BLOCK)
    columns[...] = first.astype(jnp.int32) + offset
    here = lax.axis_index("seg")
    after = lax.rem(here + 1, lax.axis_size("seg"))
    row = lax.broadcasted_iota(jnp.int32, (K, K), 0)
    for segment, out in ((here, order_here), (after, order_next)):
        out[...] = jnp.where(row == columns[pl.ds(segment, 1), :], 1.0, 0.0).astype(jnp.bfloat16)


def near_kernel(
    counts, own_first, own_second, first, second, own_coefs, near_coefs, level0, level1, level2, level3
):
    odd = core_is_odd()
    zs = own_coefs.shape[2]
    ys = own_coefs.shape[0] // 4

    def fill(k, _):
        backward = jnp.where(odd, 1 - k, k)
        unpack_layer(second, backward, ys, level0, 3 - k)
        unpack_layer(first, backward, ys, level0, 1 - k)
        forward = jnp.where(odd, k, 1 - k)
        unpack_layer(own_second, forward, ys, level0, 4 + k)
        unpack_layer(own_first, forward, ys, level0, 6 + k)
        return 0

    lax.fori_loop(0, 2, fill, 0)
    levels = (level0, level1, level2, level3)
    for t, layers in enumerate(NEAR_LAYERS):
        source, dest = levels[t], levels[t + 1]
        active = None if t < 2 else counts[0] > t
        half = layers // 2

        def one(j, coefs, layer):
            refs = [(source, j + k) for k in range(3)]
            step_layer(*refs, coefs, layer, active, into_level(dest, j, zs))

        def near_one(j, _):
            one(j, near_coefs, j + t)
            return 0

        def own_one(j, _):
            one(half + j, own_coefs, j)
            return 0

        lax.fori_loop(0, half, near_one, 0)
        lax.fori_loop(0, half, own_one, 0)


def two_layers(counts, befores, news, coefs_of, image, places):
    zs = image.shape[2]
    for t in range(STEPS):
        before, new = befores[t], news[t]
        end = before.shape[0]
        active = None if t < 2 else counts[0] > t
        window = ((before, end - 2), (before, end - 1), (new, 0), (new, 1))
        for j in range(2):
            if t < STEPS - 1:
                store = into_level(news[t + 1], j, zs)
            else:
                place = places[j]

                def store(y, h, z, rows):
                    image[place, y, z : z + CHUNK, h * HALF : (h + 1) * HALF] = rows

            step_layer(*window[j : j + 3], *coefs_of(t, j), active, store)


def fill_pair(source, dest, ys):
    odd = core_is_odd()

    def fill(k, _):
        unpack_layer(source, jnp.where(odd, k, 1 - k), ys, dest, k)
        return 0

    lax.fori_loop(0, 2, fill, 0)


def first_kernel(
    counts, first, own_coefs, near0, near1, near2, near3,
    image, far_coefs, level0, level1, level2, level3, far_fields, table,
):
    ys = image.shape[1]
    unpack_fields(first, far_fields)
    columns = coef_columns(far_fields, ys, core_is_odd(), True, table)
    for k in range(3):
        for y in range(ys):
            spread_coefs(columns, ((3 - k) * ys + y) * FIELDS, far_coefs, k * ys + y)
    fill_pair(first, level0, ys)

    def coefs_of(t, j):
        u = 3 - t + j
        return (own_coefs, u) if u < 4 else (far_coefs, u - 4)

    odd = core_is_odd()
    places = [jnp.where(odd, j, 1 - j) for j in range(2)]
    two_layers(counts, (near0, near1, near2, near3), (level0, level1, level2, level3), coefs_of, image, places)


def second_kernel(
    counts, second, done, own_coefs, far_coefs, near0, near1, near2, near3, image, level0, level1, level2, level3
):
    ys = image.shape[1]
    start = jnp.where(core_is_odd(), 0, 2)
    for k in range(2):
        image[start + k] = done[k]
    fill_pair(second, level0, ys)

    def coefs_of(t, j):
        u = 5 - t + j
        return (own_coefs, u) if u < 4 else (far_coefs, u - 4)

    odd = core_is_odd()
    places = [jnp.where(odd, 2 + j, 1 - j) for j in range(2)]
    two_layers(counts, (near0, near1, near2, near3), (level0, level1, level2, level3), coefs_of, image, places)


def mul(left, right):
    return jnp.dot(left, right, preferred_element_type=jnp.float32)


def to_bf16(value):
    return value.astype(jnp.bfloat16)


def to_f32(value):
    return value.astype(jnp.float32)


def product_kernel(ahead, state, order_next, order_here, image, out, sem):
    save = pltpu.make_async_copy(state, image, sem)
    save.start()
    left = ahead[...].reshape(-1, K)
    right = state[...].reshape(-1, K)
    raw = lax.dot_general(left, right, (((0,), (0,)), ((), ())), preferred_element_type=jnp.float32)
    raw = to_bf16(mul(order_next[...], to_bf16(raw)))
    turned = (((1,), (1,)), ((), ()))
    out[...] = to_bf16(lax.dot_general(raw, order_here[...], turned, preferred_element_type=jnp.float32))
    save.wait()


def specs(kinds):
    spaces = {"s": pltpu.SMEM, "v": pltpu.VMEM, "a": pl.ANY, "h": pltpu.HBM}
    return [pl.BlockSpec(memory_space=spaces[kind]) for kind in kinds]


def params(megabytes):
    return pltpu.CompilerParams(vmem_limit_bytes=megabytes * 2**20)


def cost(flops, read):
    return pl.CostEstimate(flops=int(flops), bytes_accessed=int(read), transcendentals=0)


def pinned(value):
    return pltpu.with_memory_space_constraint(value, pltpu.HBM)


def pack(start, diffusivity, velocity):
    planes, zs = start.shape[0], start.shape[1]
    rows = diffusivity.shape[0] * diffusivity.shape[1] * FIELDS
    return pl.pallas_call(
        pack_kernel,
        out_shape=(
            jax.ShapeDtypeStruct((planes // 2 + 1, zs, K), jnp.bfloat16),
            jax.ShapeDtypeStruct((planes // 2, zs, K), jnp.bfloat16),
            jax.ShapeDtypeStruct((rows, zs), jnp.float32),
        ),
        in_specs=specs("hhh"),
        out_specs=tuple(specs("vvv")),
        scratch_shapes=[
            pltpu.VMEM(diffusivity.shape, jnp.float32),
            pltpu.VMEM(velocity.shape, jnp.float32),
            pltpu.SemaphoreType.DMA((4,)),
        ],
        compiler_params=params(8),
        cost_estimate=cost(0, 0),
    )(pinned(start), pinned(diffusivity), pinned(velocity))


def factors(layers, ys, zs):
    return jax.ShapeDtypeStruct((layers * ys, 7, zs, HALF), jnp.float32)


def level_shape(layers, ys):
    return jax.ShapeDtypeStruct((layers, ys, 2, ROWS, HALF), jnp.float32)


def spread(fields, near_first, order, ys):
    zs = fields.shape[1]
    perm = jax.ShapeDtypeStruct((K, K), jnp.bfloat16)
    return pl.pallas_call(
        coefs_kernel,
        out_shape=(factors(4, ys, zs), factors(3, ys, zs), perm, perm),
        in_specs=specs("vvh"),
        out_specs=tuple(specs("vvvv")),
        scratch_shapes=[
            pltpu.VMEM(fields.shape, jnp.float32),
            pltpu.VMEM((128, zs), jnp.float32),
            pltpu.VMEM(order.shape, jnp.int32),
            pltpu.VMEM((order.shape[0], K), jnp.int32),
            pltpu.SemaphoreType.DMA,
        ],
        compiler_params=params(8),
        cost_estimate=cost(0, 0),
    )(fields, near_first, pinned(order))


def near_steps(counts, own_first, own_second, first, second, own_coefs, near_coefs, ys):
    return pl.pallas_call(
        near_kernel,
        out_shape=tuple(level_shape(layers, ys) for layers in (8, *NEAR_LAYERS)),
        in_specs=specs("svvvvvv"),
        out_specs=tuple(specs("vvvv")),
        compiler_params=params(8),
        cost_estimate=cost(0, 0),
    )(counts, own_first, own_second, first, second, own_coefs, near_coefs)


def first_steps(counts, first, own_coefs, levels, shape, rows):
    ys, zs = shape[1], shape[2]
    return pl.pallas_call(
        first_kernel,
        out_shape=(
            jax.ShapeDtypeStruct((2, *shape[1:]), jnp.bfloat16),
            factors(3, ys, zs),
            *[level_shape(2, ys)] * 4,
        ),
        in_specs=specs("svvvvvv"),
        out_specs=tuple(specs("vvvvvv")),
        scratch_shapes=[pltpu.VMEM((rows, zs), jnp.float32), pltpu.VMEM((128, zs), jnp.float32)],
        compiler_params=params(8),
        cost_estimate=cost(0, 0),
    )(counts, first, own_coefs, *levels)


def second_steps(counts, second, done, own_coefs, far_coefs, levels, shape):
    ys = shape[1]
    return pl.pallas_call(
        second_kernel,
        out_shape=jax.ShapeDtypeStruct(shape, jnp.bfloat16),
        in_specs=specs("svvvvvvvv"),
        out_specs=specs("v")[0],
        scratch_shapes=[pltpu.VMEM((2, ys, 2, ROWS, HALF), jnp.float32)] * 4,
        compiler_params=params(8),
        cost_estimate=cost(0, 0),
    )(counts, second, done, own_coefs, far_coefs, *levels)


def products(ahead, state, order_next, order_here):
    return pl.pallas_call(
        product_kernel,
        out_shape=(
            jax.ShapeDtypeStruct(state.shape, state.dtype),
            jax.ShapeDtypeStruct((K, K), jnp.bfloat16),
        ),
        in_specs=specs("vvvv"),
        out_specs=tuple(specs("av")),
        scratch_shapes=[pltpu.SemaphoreType.DMA],
        compiler_params=params(16),
        cost_estimate=cost(0, 0),
    )(ahead, state, order_next, order_here)


def mixed_swap(value, along, across, core_along):
    total, slabs = lax.axis_size("seg"), lax.axis_size("space")
    route = []
    for s in range(total):
        for x in range(slabs):
            if core_along:
                to = (s ^ along, x) if x % 2 else (s, x ^ across)
            else:
                to = (s ^ along, x ^ across)
            route.append((s * slabs + x, to[0] * slabs + to[1]))
    return lax.ppermute(value, ("seg", "space"), route)


def per_device(basis, diffusivity, velocity, step_counts, block_order):
    start = basis[0]
    total = lax.axis_size("seg")
    slabs = lax.axis_size("space")
    cells = start.shape[0] * slabs * start.shape[1] * start.shape[2]

    ahead = lax.ppermute(start, "seg", [((i + 1) % total, i) for i in range(total)])
    ys, zs = start.shape[1], start.shape[2]
    planes = start.reshape(-1, zs, K)
    first, second, fields = pack(planes, diffusivity[0].transpose(1, 0, 2), velocity[0].transpose(0, 2, 1, 3))
    near_first = exchange_pairs(first, "space", 0)
    near_second = exchange_pairs(second, "space", 0)
    far_first = exchange_pairs(first, "space", 1)
    far_second = exchange_pairs(second, "space", 1)
    own_coefs, near_coefs, order_here, order_next = spread(fields, near_first, block_order, ys)
    levels = near_steps(step_counts, first, second, near_first, near_second, own_coefs, near_coefs, ys)
    image_first, far_coefs, *levels = first_steps(
        step_counts, far_first, own_coefs, levels, start.shape, fields.shape[0]
    )
    state = second_steps(step_counts, far_second, image_first, own_coefs, far_coefs, levels, start.shape)
    image, raw = products(ahead, state, order_next, order_here)

    bit = 1
    while 2 * bit < slabs:
        raw = to_bf16(to_f32(raw) + to_f32(swap(raw, "space", bit)))
        bit *= 2
    odd = lax.axis_index("space") % 2 == 1

    def my_half(full):
        return jnp.where(odd, full[:, HALF:], full[:, :HALF])

    def both_halves(part):
        rest = swap(part, "space", 1)
        return jnp.where(odd, jnp.concatenate([rest, part], 1), jnp.concatenate([part, rest], 1))

    straight = mixed_swap(raw, 1, bit, True)
    diagonal = mixed_swap(my_half(raw), 1, bit, False)
    straight_other = swap(straight, "space", 1)
    diagonal_other = swap(diagonal, "space", 1)
    scale = coupling / math.sqrt(K * cells)
    across = jnp.where(odd, straight_other, straight)
    along = jnp.where(odd, straight, straight_other)
    diagonal = jnp.where(odd, jnp.concatenate([diagonal_other, diagonal], 1), jnp.concatenate([diagonal, diagonal_other], 1))
    mine = to_bf16((to_f32(raw) + to_f32(across)) * scale)
    theirs = to_bf16((to_f32(along) + to_f32(diagonal)) * scale)
    def chained(later, earlier):
        return to_f32(later) + to_f32(earlier) + mul(later, earlier)

    upper = lax.axis_index("seg") % 2 == 1
    later = jnp.where(upper, mine, theirs)
    earlier = jnp.where(upper, theirs, mine)
    half = to_bf16(to_f32(my_half(later)) + to_f32(my_half(earlier)) + mul(later, my_half(earlier)))
    block = chained(later, earlier)
    wide = jnp.where(upper, block, to_f32(mine))
    bit = 2
    while bit < total:
        upper = (lax.axis_index("seg") // bit) % 2 == 1
        got = both_halves(swap(half, "seg", bit))
        wide = jnp.where(upper, wide + to_f32(got) + mul(to_bf16(wide), got), wide)
        block = to_bf16(block)
        later = jnp.where(upper, block, got)
        earlier = jnp.where(upper, got, block)
        block = chained(later, earlier)
        half = to_bf16(my_half(block))
        bit *= 2
    monodromy = wide + jnp.eye(K, dtype=jnp.float32)
    return (image[None], monodromy[None])


def solution(mesh):
    in_specs = (
        P(("groups", "seg"), "space", None, None, None),
        P(("groups", "seg"), "space", None, None),
        P(("groups", "seg"), None, "space", None, None),
        P(("groups", "seg")),
        P("groups", None),
    )
    out_specs = (P(("groups", "seg"), "space", None, None, None), P(("groups", "seg"), None, None))
    return jax.shard_map(
        per_device, mesh=mesh, in_specs=in_specs, out_specs=out_specs, check_vma=False
    )
```

```python
import math

import jax
import jax.numpy as jnp
from jax import lax
from jax.experimental import pallas as pl
from jax.experimental.pallas import tpu as pltpu
from jax.sharding import PartitionSpec as P

K = 256
BLOCK = 16
STEPS = 4
HALF = K // 2

coupling = 0.35


def swap(value, axis, bit):
    size = lax.axis_size(axis)
    return lax.ppermute(value, axis, [(i, i ^ bit) for i in range(size)])


def exchange_pairs(value, axis, first):
    size = lax.axis_size(axis)
    route = []
    for i in range(first, size - 1, 2):
        route += [(i, i + 1), (i + 1, i)]
    return lax.ppermute(value, axis, route)


ROWS = 144
TOP = 8
CHUNK = 16
FIELDS = 4
NEAR_LAYERS = (6, 4, 2)


def spread_coefs(columns, column, out, plane):
    def field(k):
        return jnp.broadcast_to(columns[:, column + k : column + k + 1], (columns.shape[0], HALF))

    diffusion = field(0)
    along_u = field(1)
    along_y = field(2)
    along_z = field(3)
    out[plane, 0] = 1.0 - 6.0 * diffusion
    out[plane, 1] = diffusion - along_u
    out[plane, 2] = diffusion + along_u
    out[plane, 3] = diffusion - along_y
    out[plane, 4] = diffusion + along_y
    out[plane, 5] = diffusion - along_z
    out[plane, 6] = diffusion + along_z


def coef_columns(fields, ys, odd, backward, table):
    layers = fields.shape[0] // (ys * FIELDS)
    table[...] = jnp.zeros_like(table)
    sign = jnp.where(odd, 0.5, -0.5)
    for k in range(layers):
        flipped = layers - 1 - k
        x = jnp.where(odd, flipped, k) if backward else jnp.where(odd, k, flipped)
        for y in range(ys):
            for f in range(FIELDS):
                row = fields[pl.ds((f * ys + y) * layers + x, 1), :]
                if f == 1:
                    row = row * sign
                elif f > 1:
                    row = row * 0.5
                at = (k * ys + y) * FIELDS + f
                table[at : at + 1, :] = row
    return table[...].T


def unpack_layer(source, index, ys, dest, slot):
    zs = source.shape[1]
    for y in range(ys):
        for h in range(2):
            value = source[index * ys + y, :, h * HALF : (h + 1) * HALF].astype(jnp.float32)
            dest[slot, y, h, TOP : TOP + zs, :] = value
            dest[slot, y, h, TOP - 1 : TOP, :] = value[zs - 1 : zs]
            dest[slot, y, h, TOP + zs : TOP + zs + 1, :] = value[0:1]


def step_layer(minus, here, plus, coefs, layer, active, store):
    level, slot = here
    ys = level.shape[1]
    zs = coefs.shape[2]
    for z in range(0, zs, CHUNK):
        rows = slice(TOP + z, TOP + z + CHUNK)
        centers = [[level[slot, y, h, rows, :] for h in range(2)] for y in range(ys)]
        for y in range(ys):
            factor = [coefs[layer * ys + y, k, z : z + CHUNK, :] for k in range(7)]
            for h in range(2):
                center = centers[y][h]
                new = factor[0] * center
                new += factor[1] * plus[0][plus[1], y, h, rows, :]
                new += factor[2] * minus[0][minus[1], y, h, rows, :]
                new += factor[3] * centers[(y + 1) % ys][h]
                new += factor[4] * centers[(y + ys - 1) % ys][h]
                new += factor[5] * level[slot, y, h, TOP + z + 1 : TOP + z + CHUNK + 1, :]
                new += factor[6] * level[slot, y, h, TOP + z - 1 : TOP + z + CHUNK - 1, :]
                if active is not None:
                    new = jnp.where(active, new, center)
                store(y, h, z, new.astype(jnp.bfloat16))


def into_level(dest, slot, zs):
    def store(y, h, z, rows):
        wide = rows.astype(jnp.float32)
        dest[slot, y, h, TOP + z : TOP + z + CHUNK, :] = wide
        if z == 0:
            dest[slot, y, h, TOP + zs : TOP + zs + 1, :] = wide[0:1]
        if z + CHUNK == zs:
            dest[slot, y, h, TOP - 1 : TOP, :] = wide[CHUNK - 1 : CHUNK]

    return store


def core_is_odd():
    return lax.axis_index("space") % 2 == 1


def pack_kernel(start, diffusivity, velocity, first, second, fields, spread_home, drift_home, sems):
    odd = core_is_odd()
    half = second.shape[0]
    here = jnp.where(odd, half, 0)
    there = jnp.where(odd, 0, half)
    small = (
        pltpu.make_async_copy(diffusivity, spread_home, sems.at[0]),
        pltpu.make_async_copy(velocity, drift_home, sems.at[1]),
    )
    copies = (
        pltpu.make_async_copy(start.at[pl.ds(here, half)], first.at[pl.ds(0, half)], sems.at[2]),
        pltpu.make_async_copy(start.at[pl.ds(there, half)], second, sems.at[3]),
    )
    for copy in small + copies:
        copy.start()
    for copy in small:
        copy.wait()
    ys, layers = spread_home.shape[0], spread_home.shape[1]
    for y in range(ys):
        for f in range(FIELDS):
            at = (f * ys + y) * layers
            fields[at : at + layers, :] = spread_home[y] if f == 0 else drift_home[f - 1, y]
    value = fields[...]
    high = to_bf16(value)
    rest = value - to_f32(high)
    middle = to_bf16(rest)
    low = to_bf16(rest - to_f32(middle))
    rows = value.shape[0]
    first[half, :rows, :HALF] = high
    first[half, :rows, HALF:] = middle
    first[half, rows : 2 * rows, :HALF] = low
    first[half, rows : 2 * rows, HALF:] = jnp.zeros_like(low)
    if first.shape[1] > 2 * rows:
        first[half, 2 * rows :, :] = jnp.zeros((first.shape[1] - 2 * rows, K), jnp.bfloat16)
    for copy in copies:
        copy.wait()


def unpack_fields(packed, fields):
    rows = fields.shape[0]
    at = packed.shape[0] - 1
    high = to_f32(packed[at, :rows, :HALF])
    middle = to_f32(packed[at, :rows, HALF:])
    low = to_f32(packed[at, rows : 2 * rows, :HALF])
    fields[...] = high + (middle + low)


def coefs_kernel(
    own_fields, near_first, order_home, own_coefs, near_coefs, order_here, order_next,
    near_fields, table, order, columns, sem,
):
    fetch = pltpu.make_async_copy(order_home, order, sem)
    fetch.start()
    odd = core_is_odd()
    ys = own_coefs.shape[0] // 4
    unpack_fields(near_first, near_fields)
    turned = coef_columns(own_fields, ys, odd, False, table)
    for u in range(4):
        for y in range(ys):
            spread_coefs(turned, (u * ys + y) * FIELDS, own_coefs, u * ys + y)
    turned = coef_columns(near_fields, ys, odd, True, table)
    for k in range(3):
        for y in range(ys):
            spread_coefs(turned, (k * ys + y) * FIELDS, near_coefs, (2 - k) * ys + y)

    fetch.wait()
    segments, blocks = order.shape
    block = lax.broadcasted_iota(jnp.int32, (blocks, K), 0)
    stored = lax.broadcasted_iota(jnp.int32, (blocks, K), 1)
    inside = jnp.where(lax.div(stored, BLOCK) == block, float(BLOCK), 0.0).astype(jnp.bfloat16)
    first = mul(order[...].astype(jnp.float32).astype(jnp.bfloat16), inside)
    offset = lax.rem(lax.broadcasted_iota(jnp.int32, first.shape, 1), BLOCK)
    columns[...] = first.astype(jnp.int32) + offset
    here = lax.axis_index("seg")
    after = lax.rem(here + 1, lax.axis_size("seg"))
    row = lax.broadcasted_iota(jnp.int32, (K, K), 0)
    for segment, out in ((here, order_here), (after, order_next)):
        out[...] = jnp.where(row == columns[pl.ds(segment, 1), :], 1.0, 0.0).astype(jnp.bfloat16)


def near_kernel(
    counts, own_first, own_second, first, second, own_coefs, near_coefs, level0, level1, level2, level3
):
    odd = core_is_odd()
    zs = own_coefs.shape[2]
    ys = own_coefs.shape[0] // 4

    def fill(k, _):
        backward = jnp.where(odd, 1 - k, k)
        unpack_layer(second, backward, ys, level0, 3 - k)
        unpack_layer(first, backward, ys, level0, 1 - k)
        forward = jnp.where(odd, k, 1 - k)
        unpack_layer(own_second, forward, ys, level0, 4 + k)
        unpack_layer(own_first, forward, ys, level0, 6 + k)
        return 0

    lax.fori_loop(0, 2, fill, 0)
    levels = (level0, level1, level2, level3)
    for t, layers in enumerate(NEAR_LAYERS):
        source, dest = levels[t], levels[t + 1]
        active = None if t < 2 else counts[0] > t
        half = layers // 2

        def one(j, coefs, layer):
            refs = [(source, j + k) for k in range(3)]
            step_layer(*refs, coefs, layer, active, into_level(dest, j, zs))

        def near_one(j, _):
            one(j, near_coefs, j + t)
            return 0

        def own_one(j, _):
            one(half + j, own_coefs, j)
            return 0

        lax.fori_loop(0, half, near_one, 0)
        lax.fori_loop(0, half, own_one, 0)


def two_layers(counts, befores, news, coefs_of, image, places):
    zs = image.shape[2]
    for t in range(STEPS):
        before, new = befores[t], news[t]
        end = before.shape[0]
        active = None if t < 2 else counts[0] > t
        window = ((before, end - 2), (before, end - 1), (new, 0), (new, 1))
        for j in range(2):
            if t < STEPS - 1:
                store = into_level(news[t + 1], j, zs)
            else:
                place = places[j]

                def store(y, h, z, rows):
                    image[place, y, z : z + CHUNK, h * HALF : (h + 1) * HALF] = rows

            step_layer(*window[j : j + 3], *coefs_of(t, j), active, store)


def fill_pair(source, dest, ys):
    odd = core_is_odd()

    def fill(k, _):
        unpack_layer(source, jnp.where(odd, k, 1 - k), ys, dest, k)
        return 0

    lax.fori_loop(0, 2, fill, 0)


def first_kernel(
    counts, first, own_coefs, near0, near1, near2, near3,
    image, far_coefs, level0, level1, level2, level3, far_fields, table,
):
    ys = image.shape[1]
    unpack_fields(first, far_fields)
    columns = coef_columns(far_fields, ys, core_is_odd(), True, table)
    for k in range(3):
        for y in range(ys):
            spread_coefs(columns, ((3 - k) * ys + y) * FIELDS, far_coefs, k * ys + y)
    fill_pair(first, level0, ys)

    def coefs_of(t, j):
        u = 3 - t + j
        return (own_coefs, u) if u < 4 else (far_coefs, u - 4)

    odd = core_is_odd()
    places = [jnp.where(odd, j, 1 - j) for j in range(2)]
    two_layers(counts, (near0, near1, near2, near3), (level0, level1, level2, level3), coefs_of, image, places)


def second_kernel(
    counts, second, done, own_coefs, far_coefs, near0, near1, near2, near3, image, level0, level1, level2, level3
):
    ys = image.shape[1]
    start = jnp.where(core_is_odd(), 0, 2)
    for k in range(2):
        image[start + k] = done[k]
    fill_pair(second, level0, ys)

    def coefs_of(t, j):
        u = 5 - t + j
        return (own_coefs, u) if u < 4 else (far_coefs, u - 4)

    odd = core_is_odd()
    places = [jnp.where(odd, 2 + j, 1 - j) for j in range(2)]
    two_layers(counts, (near0, near1, near2, near3), (level0, level1, level2, level3), coefs_of, image, places)


def mul(left, right):
    return jnp.dot(left, right, preferred_element_type=jnp.float32)


def to_bf16(value):
    return value.astype(jnp.bfloat16)


def to_f32(value):
    return value.astype(jnp.float32)


def save_kernel(state, image, sem):
    save = pltpu.make_async_copy(state, image, sem)
    save.start()
    save.wait()


def product_kernel(ahead, state, order_next, order_here, out):
    left = ahead[...].reshape(-1, K)
    right = state[...].reshape(-1, K)
    raw = lax.dot_general(left, right, (((0,), (0,)), ((), ())), preferred_element_type=jnp.float32)
    raw = to_bf16(mul(order_next[...], to_bf16(raw)))
    turned = (((1,), (1,)), ((), ()))
    out[...] = to_bf16(lax.dot_general(raw, order_here[...], turned, preferred_element_type=jnp.float32))


def specs(kinds):
    spaces = {"s": pltpu.SMEM, "v": pltpu.VMEM, "a": pl.ANY, "h": pltpu.HBM}
    return [pl.BlockSpec(memory_space=spaces[kind]) for kind in kinds]


def params(megabytes):
    return pltpu.CompilerParams(vmem_limit_bytes=megabytes * 2**20)


def cost(flops, read):
    return pl.CostEstimate(flops=int(flops), bytes_accessed=int(read), transcendentals=0)


def pinned(value):
    return pltpu.with_memory_space_constraint(value, pltpu.HBM)


def pack(start, diffusivity, velocity):
    planes, zs = start.shape[0], start.shape[1]
    rows = diffusivity.shape[0] * diffusivity.shape[1] * FIELDS
    return pl.pallas_call(
        pack_kernel,
        out_shape=(
            jax.ShapeDtypeStruct((planes // 2 + 1, zs, K), jnp.bfloat16),
            jax.ShapeDtypeStruct((planes // 2, zs, K), jnp.bfloat16),
            jax.ShapeDtypeStruct((rows, zs), jnp.float32),
        ),
        in_specs=specs("hhh"),
        out_specs=tuple(specs("vvv")),
        scratch_shapes=[
            pltpu.VMEM(diffusivity.shape, jnp.float32),
            pltpu.VMEM(velocity.shape, jnp.float32),
            pltpu.SemaphoreType.DMA((4,)),
        ],
        compiler_params=params(8),
        cost_estimate=cost(0, 0),
    )(pinned(start), pinned(diffusivity), pinned(velocity))


def factors(layers, ys, zs):
    return jax.ShapeDtypeStruct((layers * ys, 7, zs, HALF), jnp.float32)


def level_shape(layers, ys):
    return jax.ShapeDtypeStruct((layers, ys, 2, ROWS, HALF), jnp.float32)


def spread(fields, near_first, order, ys):
    zs = fields.shape[1]
    perm = jax.ShapeDtypeStruct((K, K), jnp.bfloat16)
    return pl.pallas_call(
        coefs_kernel,
        out_shape=(factors(4, ys, zs), factors(3, ys, zs), perm, perm),
        in_specs=specs("vvh"),
        out_specs=tuple(specs("vvvv")),
        scratch_shapes=[
            pltpu.VMEM(fields.shape, jnp.float32),
            pltpu.VMEM((128, zs), jnp.float32),
            pltpu.VMEM(order.shape, jnp.int32),
            pltpu.VMEM((order.shape[0], K), jnp.int32),
            pltpu.SemaphoreType.DMA,
        ],
        compiler_params=params(8),
        cost_estimate=cost(0, 0),
    )(fields, near_first, pinned(order))


def near_steps(counts, own_first, own_second, first, second, own_coefs, near_coefs, ys):
    return pl.pallas_call(
        near_kernel,
        out_shape=tuple(level_shape(layers, ys) for layers in (8, *NEAR_LAYERS)),
        in_specs=specs("svvvvvv"),
        out_specs=tuple(specs("vvvv")),
        compiler_params=params(8),
        cost_estimate=cost(0, 0),
    )(counts, own_first, own_second, first, second, own_coefs, near_coefs)


def first_steps(counts, first, own_coefs, levels, shape, rows):
    ys, zs = shape[1], shape[2]
    return pl.pallas_call(
        first_kernel,
        out_shape=(
            jax.ShapeDtypeStruct((2, *shape[1:]), jnp.bfloat16),
            factors(3, ys, zs),
            *[level_shape(2, ys)] * 4,
        ),
        in_specs=specs("svvvvvv"),
        out_specs=tuple(specs("vvvvvv")),
        scratch_shapes=[pltpu.VMEM((rows, zs), jnp.float32), pltpu.VMEM((128, zs), jnp.float32)],
        compiler_params=params(8),
        cost_estimate=cost(0, 0),
    )(counts, first, own_coefs, *levels)


def second_steps(counts, second, done, own_coefs, far_coefs, levels, shape):
    ys = shape[1]
    return pl.pallas_call(
        second_kernel,
        out_shape=jax.ShapeDtypeStruct(shape, jnp.bfloat16),
        in_specs=specs("svvvvvvvv"),
        out_specs=specs("v")[0],
        scratch_shapes=[pltpu.VMEM((2, ys, 2, ROWS, HALF), jnp.float32)] * 4,
        compiler_params=params(8),
        cost_estimate=cost(0, 0),
    )(counts, second, done, own_coefs, far_coefs, *levels)


def products(ahead, state, order_next, order_here):
    return pl.pallas_call(
        product_kernel,
        out_shape=jax.ShapeDtypeStruct((K, K), jnp.bfloat16),
        in_specs=specs("vvvv"),
        out_specs=specs("v")[0],
        compiler_params=params(16),
        cost_estimate=cost(0, 0),
    )(ahead, state, order_next, order_here)


def save(state):
    return pl.pallas_call(
        save_kernel,
        out_shape=jax.ShapeDtypeStruct(state.shape, state.dtype),
        in_specs=specs("v"),
        out_specs=specs("a")[0],
        scratch_shapes=[pltpu.SemaphoreType.DMA],
        compiler_params=params(4),
        cost_estimate=cost(0, 2 * state.size * state.dtype.itemsize),
    )(state)


def mixed_swap(value, along, across, core_along):
    total, slabs = lax.axis_size("seg"), lax.axis_size("space")
    route = []
    for s in range(total):
        for x in range(slabs):
            if core_along:
                to = (s ^ along, x) if x % 2 else (s, x ^ across)
            else:
                to = (s ^ along, x ^ across)
            route.append((s * slabs + x, to[0] * slabs + to[1]))
    return lax.ppermute(value, ("seg", "space"), route)


def per_device(basis, diffusivity, velocity, step_counts, block_order):
    start = basis[0]
    total = lax.axis_size("seg")
    slabs = lax.axis_size("space")
    cells = start.shape[0] * slabs * start.shape[1] * start.shape[2]

    ahead = lax.ppermute(start, "seg", [((i + 1) % total, i) for i in range(total)])
    ys, zs = start.shape[1], start.shape[2]
    planes = start.reshape(-1, zs, K)
    first, second, fields = pack(planes, diffusivity[0].transpose(1, 0, 2), velocity[0].transpose(0, 2, 1, 3))
    near_first = exchange_pairs(first, "space", 0)
    near_second = exchange_pairs(second, "space", 0)
    far_first = exchange_pairs(first, "space", 1)
    far_second = exchange_pairs(second, "space", 1)
    own_coefs, near_coefs, order_here, order_next = spread(fields, near_first, block_order, ys)
    levels = near_steps(step_counts, first, second, near_first, near_second, own_coefs, near_coefs, ys)
    image_first, far_coefs, *levels = first_steps(
        step_counts, far_first, own_coefs, levels, start.shape, fields.shape[0]
    )
    state = second_steps(step_counts, far_second, image_first, own_coefs, far_coefs, levels, start.shape)
    raw = products(ahead, state, order_next, order_here)

    bit = 1
    while 2 * bit < slabs:
        raw = to_bf16(to_f32(raw) + to_f32(swap(raw, "space", bit)))
        bit *= 2
    odd = lax.axis_index("space") % 2 == 1
    upper = lax.axis_index("seg") % 2 == 1

    def my_half(full):
        return jnp.where(odd, full[:, HALF:], full[:, :HALF])

    def my_rows(full):
        return jnp.where(odd, full[HALF:], full[:HALF])

    def folded(rows):
        return jnp.concatenate([rows[:, :HALF], rows[:, HALF:]], 0)

    def unfolded(part):
        return jnp.concatenate([part[:HALF], part[HALF:]], 1)

    def both_halves(part):
        rest = swap(part, "space", 1)
        return jnp.where(odd, jnp.concatenate([rest, part], 1), jnp.concatenate([part, rest], 1))

    def both_parts(part):
        rest = swap(part, "space", 1)
        low = jnp.where(odd, rest, part)
        high = jnp.where(odd, part, rest)
        rows = jnp.concatenate([unfolded(low), unfolded(high)], 0)
        return jnp.where(upper, jnp.concatenate([low, high], 1), rows)

    def chained(later, earlier):
        return to_f32(later) + to_f32(earlier) + mul(later, earlier)

    scale = coupling / math.sqrt(K * cells)

    def factor(one, two):
        return to_bf16((to_f32(one) + to_f32(two)) * scale)

    straight = mixed_swap(raw, 1, bit, True)
    diagonal = mixed_swap(jnp.where(upper, folded(my_rows(raw)), my_half(raw)), 1, bit, False)
    straight_other = swap(straight, "space", 1)
    across = jnp.where(odd, straight_other, straight)
    along = jnp.where(odd, straight, straight_other)
    mine = factor(raw, across)
    columns = factor(my_half(along), diagonal)
    rows = factor(my_rows(along), unfolded(diagonal))
    up = to_f32(my_half(mine)) + to_f32(columns) + mul(mine, columns)
    down = to_f32(my_rows(mine)) + to_f32(rows) + mul(rows, mine)
    half = jnp.where(upper, to_bf16(up), folded(to_bf16(down)))
    got_part = swap(half, "seg", 2) if total > 2 else None

    state, diagonal, half = lax.optimization_barrier((state, diagonal, half))
    image = save(state)
    theirs = factor(along, both_parts(diagonal))
    block = chained(jnp.where(upper, mine, theirs), jnp.where(upper, theirs, mine))
    wide = jnp.where(upper, block, to_f32(mine))
    bit = 2
    while bit < total:
        higher = (lax.axis_index("seg") // bit) % 2 == 1
        block = to_bf16(block)
        got = both_parts(got_part) if bit == 2 else both_halves(swap(my_half(block), "seg", bit))
        wide = jnp.where(higher, wide + to_f32(got) + mul(to_bf16(wide), got), wide)
        if 2 * bit < total:
            block = chained(jnp.where(higher, block, got), jnp.where(higher, got, block))
        bit *= 2
    monodromy = wide + jnp.eye(K, dtype=jnp.float32)
    return (image[None], monodromy[None])


def solution(mesh):
    in_specs = (
        P(("groups", "seg"), "space", None, None, None),
        P(("groups", "seg"), "space", None, None),
        P(("groups", "seg"), None, "space", None, None),
        P(("groups", "seg")),
        P("groups", None),
    )
    out_specs = (P(("groups", "seg"), "space", None, None, None), P(("groups", "seg"), None, None))
    return jax.shard_map(
        per_device, mesh=mesh, in_specs=in_specs, out_specs=out_specs, check_vma=False
    )
```

```python
import math

import jax
import jax.numpy as jnp
from jax import lax
from jax.experimental import pallas as pl
from jax.experimental.pallas import tpu as pltpu
from jax.sharding import PartitionSpec as P

K = 256
BLOCK = 16
STEPS = 4
HALF = K // 2

coupling = 0.35


def swap(value, axis, bit):
    size = lax.axis_size(axis)
    return lax.ppermute(value, axis, [(i, i ^ bit) for i in range(size)])


def exchange_pairs(value, axis, first):
    size = lax.axis_size(axis)
    route = []
    for i in range(first, size - 1, 2):
        route += [(i, i + 1), (i + 1, i)]
    return lax.ppermute(value, axis, route)


ROWS = 144
TOP = 8
CHUNK = 16
FIELDS = 4
NEAR_LAYERS = (6, 4, 2)


def spread_coefs(columns, column, out, plane):
    def field(k):
        return jnp.broadcast_to(columns[:, column + k : column + k + 1], (columns.shape[0], HALF))

    diffusion = field(0)
    along_u = field(1)
    along_y = field(2)
    along_z = field(3)
    out[plane, 0] = 1.0 - 6.0 * diffusion
    out[plane, 1] = diffusion - along_u
    out[plane, 2] = diffusion + along_u
    out[plane, 3] = diffusion - along_y
    out[plane, 4] = diffusion + along_y
    out[plane, 5] = diffusion - along_z
    out[plane, 6] = diffusion + along_z


def coef_columns(fields, ys, odd, backward, table):
    layers = fields.shape[0] // (ys * FIELDS)
    table[...] = jnp.zeros_like(table)
    sign = jnp.where(odd, 0.5, -0.5)
    for k in range(layers):
        flipped = layers - 1 - k
        x = jnp.where(odd, flipped, k) if backward else jnp.where(odd, k, flipped)
        for y in range(ys):
            for f in range(FIELDS):
                row = fields[pl.ds((f * ys + y) * layers + x, 1), :]
                if f == 1:
                    row = row * sign
                elif f > 1:
                    row = row * 0.5
                at = (k * ys + y) * FIELDS + f
                table[at : at + 1, :] = row
    return table[...].T


def unpack_layer(source, index, ys, dest, slot):
    zs = dest.shape[3] - 2 * TOP
    per = zs // BLOCK
    for y in range(ys):
        for h in range(2):
            value = source[pl.ds((index * ys + y) * per, per), :, h * HALF : (h + 1) * HALF]
            value = value.reshape(zs, HALF).astype(jnp.float32)
            dest[slot, y, h, TOP : TOP + zs, :] = value
            dest[slot, y, h, TOP - 1 : TOP, :] = value[zs - 1 : zs]
            dest[slot, y, h, TOP + zs : TOP + zs + 1, :] = value[0:1]


def step_layer(minus, here, plus, coefs, layer, active, store):
    level, slot = here
    ys = level.shape[1]
    zs = coefs.shape[2]
    for z in range(0, zs, CHUNK):
        rows = slice(TOP + z, TOP + z + CHUNK)
        centers = [[level[slot, y, h, rows, :] for h in range(2)] for y in range(ys)]
        for y in range(ys):
            factor = [coefs[layer * ys + y, k, z : z + CHUNK, :] for k in range(7)]
            for h in range(2):
                center = centers[y][h]
                new = factor[0] * center
                new += factor[1] * plus[0][plus[1], y, h, rows, :]
                new += factor[2] * minus[0][minus[1], y, h, rows, :]
                new += factor[3] * centers[(y + 1) % ys][h]
                new += factor[4] * centers[(y + ys - 1) % ys][h]
                new += factor[5] * level[slot, y, h, TOP + z + 1 : TOP + z + CHUNK + 1, :]
                new += factor[6] * level[slot, y, h, TOP + z - 1 : TOP + z + CHUNK - 1, :]
                if active is not None:
                    new = jnp.where(active, new, center)
                store(y, h, z, new.astype(jnp.bfloat16))


def into_level(dest, slot, zs):
    def store(y, h, z, rows):
        wide = rows.astype(jnp.float32)
        dest[slot, y, h, TOP + z : TOP + z + CHUNK, :] = wide
        if z == 0:
            dest[slot, y, h, TOP + zs : TOP + zs + 1, :] = wide[0:1]
        if z + CHUNK == zs:
            dest[slot, y, h, TOP - 1 : TOP, :] = wide[CHUNK - 1 : CHUNK]

    return store


def core_is_odd():
    return lax.axis_index("space") % 2 == 1


def pack_kernel(start, diffusivity, velocity, first, second, fields, spread_home, drift_home, sems):
    odd = core_is_odd()
    half = second.shape[0]
    here = jnp.where(odd, half, 0)
    there = jnp.where(odd, 0, half)
    small = (
        pltpu.make_async_copy(diffusivity, spread_home, sems.at[0]),
        pltpu.make_async_copy(velocity, drift_home, sems.at[1]),
    )
    copies = (
        pltpu.make_async_copy(start.at[pl.ds(here, half)], first.at[pl.ds(0, half)], sems.at[2]),
        pltpu.make_async_copy(start.at[pl.ds(there, half)], second, sems.at[3]),
    )
    for copy in small + copies:
        copy.start()
    for copy in small:
        copy.wait()
    ys, layers = spread_home.shape[0], spread_home.shape[1]
    for y in range(ys):
        for f in range(FIELDS):
            at = (f * ys + y) * layers
            fields[at : at + layers, :] = spread_home[y] if f == 0 else drift_home[f - 1, y]
    value = fields[...]
    high = to_bf16(value)
    rest = value - to_f32(high)
    middle = to_bf16(rest)
    low = to_bf16(rest - to_f32(middle))
    per = value.shape[0] // BLOCK
    shape = (per, BLOCK, HALF)
    first[half : half + per, :, :HALF] = high.reshape(shape)
    first[half : half + per, :, HALF:] = middle.reshape(shape)
    first[half + per : half + 2 * per, :, :HALF] = low.reshape(shape)
    first[half + per : half + 2 * per, :, HALF:] = jnp.zeros(shape, jnp.bfloat16)
    for copy in copies:
        copy.wait()


def unpack_fields(packed, fields):
    per = fields.shape[0] // BLOCK
    at = packed.shape[0] - 2 * per
    high = to_f32(packed[at : at + per, :, :HALF].reshape(fields.shape))
    middle = to_f32(packed[at : at + per, :, HALF:].reshape(fields.shape))
    low = to_f32(packed[at + per : at + 2 * per, :, :HALF].reshape(fields.shape))
    fields[...] = high + (middle + low)


def coefs_kernel(
    own_fields, near_first, order_home, own_coefs, near_coefs, order_here, order_next,
    near_fields, table, order, columns, sem,
):
    fetch = pltpu.make_async_copy(order_home, order, sem)
    fetch.start()
    odd = core_is_odd()
    ys = own_coefs.shape[0] // 4
    unpack_fields(near_first, near_fields)
    turned = coef_columns(own_fields, ys, odd, False, table)
    for u in range(4):
        for y in range(ys):
            spread_coefs(turned, (u * ys + y) * FIELDS, own_coefs, u * ys + y)
    turned = coef_columns(near_fields, ys, odd, True, table)
    for k in range(3):
        for y in range(ys):
            spread_coefs(turned, (k * ys + y) * FIELDS, near_coefs, (2 - k) * ys + y)

    fetch.wait()
    segments, blocks = order.shape
    block = lax.broadcasted_iota(jnp.int32, (blocks, K), 0)
    stored = lax.broadcasted_iota(jnp.int32, (blocks, K), 1)
    inside = jnp.where(lax.div(stored, BLOCK) == block, float(BLOCK), 0.0).astype(jnp.bfloat16)
    first = mul(order[...].astype(jnp.float32).astype(jnp.bfloat16), inside)
    offset = lax.rem(lax.broadcasted_iota(jnp.int32, first.shape, 1), BLOCK)
    columns[...] = first.astype(jnp.int32) + offset
    here = lax.axis_index("seg")
    after = lax.rem(here + 1, lax.axis_size("seg"))
    row = lax.broadcasted_iota(jnp.int32, (K, K), 0)
    for segment, out in ((here, order_here), (after, order_next)):
        out[...] = jnp.where(row == columns[pl.ds(segment, 1), :], 1.0, 0.0).astype(jnp.bfloat16)


def near_kernel(
    counts, own_first, own_second, first, second, own_coefs, near_coefs, level0, level1, level2, level3
):
    odd = core_is_odd()
    zs = own_coefs.shape[2]
    ys = own_coefs.shape[0] // 4

    def fill(k, _):
        backward = jnp.where(odd, 1 - k, k)
        unpack_layer(second, backward, ys, level0, 3 - k)
        unpack_layer(first, backward, ys, level0, 1 - k)
        forward = jnp.where(odd, k, 1 - k)
        unpack_layer(own_second, forward, ys, level0, 4 + k)
        unpack_layer(own_first, forward, ys, level0, 6 + k)
        return 0

    lax.fori_loop(0, 2, fill, 0)
    levels = (level0, level1, level2, level3)
    for t, layers in enumerate(NEAR_LAYERS):
        source, dest = levels[t], levels[t + 1]
        active = None if t < 2 else counts[0] > t
        half = layers // 2

        def one(j, coefs, layer):
            refs = [(source, j + k) for k in range(3)]
            step_layer(*refs, coefs, layer, active, into_level(dest, j, zs))

        def near_one(j, _):
            one(j, near_coefs, j + t)
            return 0

        def own_one(j, _):
            one(half + j, own_coefs, j)
            return 0

        lax.fori_loop(0, half, near_one, 0)
        lax.fori_loop(0, half, own_one, 0)


def two_layers(counts, befores, news, coefs_of, image, places):
    zs = image.shape[2]
    for t in range(STEPS):
        before, new = befores[t], news[t]
        end = before.shape[0]
        active = None if t < 2 else counts[0] > t
        window = ((before, end - 2), (before, end - 1), (new, 0), (new, 1))
        for j in range(2):
            if t < STEPS - 1:
                store = into_level(news[t + 1], j, zs)
            else:
                place = places[j]

                def store(y, h, z, rows):
                    image[place, y, z : z + CHUNK, h * HALF : (h + 1) * HALF] = rows

            step_layer(*window[j : j + 3], *coefs_of(t, j), active, store)


def fill_pair(source, dest, ys):
    odd = core_is_odd()

    def fill(k, _):
        unpack_layer(source, jnp.where(odd, k, 1 - k), ys, dest, k)
        return 0

    lax.fori_loop(0, 2, fill, 0)


def first_kernel(
    counts, first, own_coefs, near0, near1, near2, near3,
    image, far_coefs, level0, level1, level2, level3, far_fields, table,
):
    ys = image.shape[1]
    unpack_fields(first, far_fields)
    columns = coef_columns(far_fields, ys, core_is_odd(), True, table)
    for k in range(3):
        for y in range(ys):
            spread_coefs(columns, ((3 - k) * ys + y) * FIELDS, far_coefs, k * ys + y)
    fill_pair(first, level0, ys)

    def coefs_of(t, j):
        u = 3 - t + j
        return (own_coefs, u) if u < 4 else (far_coefs, u - 4)

    odd = core_is_odd()
    places = [jnp.where(odd, j, 1 - j) for j in range(2)]
    two_layers(counts, (near0, near1, near2, near3), (level0, level1, level2, level3), coefs_of, image, places)


def second_kernel(
    counts, second, done, own_coefs, far_coefs, near0, near1, near2, near3, image, level0, level1, level2, level3
):
    ys = image.shape[1]
    start = jnp.where(core_is_odd(), 0, 2)
    for k in range(2):
        image[start + k] = done[k]
    fill_pair(second, level0, ys)

    def coefs_of(t, j):
        u = 5 - t + j
        return (own_coefs, u) if u < 4 else (far_coefs, u - 4)

    odd = core_is_odd()
    places = [jnp.where(odd, 2 + j, 1 - j) for j in range(2)]
    two_layers(counts, (near0, near1, near2, near3), (level0, level1, level2, level3), coefs_of, image, places)


def mul(left, right):
    return jnp.dot(left, right, preferred_element_type=jnp.float32)


def to_bf16(value):
    return value.astype(jnp.bfloat16)


def to_f32(value):
    return value.astype(jnp.float32)


def save_kernel(state, image, sem):
    save = pltpu.make_async_copy(state, image, sem)
    save.start()
    save.wait()


def product_kernel(ahead, state, order_next, order_here, out):
    left = ahead[...].reshape(-1, K)
    right = state[...].reshape(-1, K)
    raw = lax.dot_general(left, right, (((0,), (0,)), ((), ())), preferred_element_type=jnp.float32)
    raw = to_bf16(mul(order_next[...], to_bf16(raw)))
    turned = (((1,), (1,)), ((), ()))
    out[...] = to_bf16(lax.dot_general(raw, order_here[...], turned, preferred_element_type=jnp.float32))


def specs(kinds):
    spaces = {"s": pltpu.SMEM, "v": pltpu.VMEM, "a": pl.ANY, "h": pltpu.HBM}
    return [pl.BlockSpec(memory_space=spaces[kind]) for kind in kinds]


def params(megabytes):
    return pltpu.CompilerParams(vmem_limit_bytes=megabytes * 2**20)


def cost(flops, read):
    return pl.CostEstimate(flops=int(flops), bytes_accessed=int(read), transcendentals=0)


def pinned(value):
    return pltpu.with_memory_space_constraint(value, pltpu.HBM)


def pack(start, diffusivity, velocity):
    planes, zs = start.shape[0], diffusivity.shape[2]
    rows = diffusivity.shape[0] * diffusivity.shape[1] * FIELDS
    return pl.pallas_call(
        pack_kernel,
        out_shape=(
            jax.ShapeDtypeStruct((planes // 2 + 2 * rows // BLOCK, BLOCK, K), jnp.bfloat16),
            jax.ShapeDtypeStruct((planes // 2, BLOCK, K), jnp.bfloat16),
            jax.ShapeDtypeStruct((rows, zs), jnp.float32),
        ),
        in_specs=specs("hhh"),
        out_specs=tuple(specs("vvv")),
        scratch_shapes=[
            pltpu.VMEM(diffusivity.shape, jnp.float32),
            pltpu.VMEM(velocity.shape, jnp.float32),
            pltpu.SemaphoreType.DMA((4,)),
        ],
        compiler_params=params(8),
        cost_estimate=cost(0, 0),
    )(pinned(start), pinned(diffusivity), pinned(velocity))


def factors(layers, ys, zs):
    return jax.ShapeDtypeStruct((layers * ys, 7, zs, HALF), jnp.float32)


def level_shape(layers, ys):
    return jax.ShapeDtypeStruct((layers, ys, 2, ROWS, HALF), jnp.float32)


def spread(fields, near_first, order, ys):
    zs = fields.shape[1]
    perm = jax.ShapeDtypeStruct((K, K), jnp.bfloat16)
    return pl.pallas_call(
        coefs_kernel,
        out_shape=(factors(4, ys, zs), factors(3, ys, zs), perm, perm),
        in_specs=specs("vvh"),
        out_specs=tuple(specs("vvvv")),
        scratch_shapes=[
            pltpu.VMEM(fields.shape, jnp.float32),
            pltpu.VMEM((128, zs), jnp.float32),
            pltpu.VMEM(order.shape, jnp.int32),
            pltpu.VMEM((order.shape[0], K), jnp.int32),
            pltpu.SemaphoreType.DMA,
        ],
        compiler_params=params(8),
        cost_estimate=cost(0, 0),
    )(fields, near_first, pinned(order))


def near_steps(counts, own_first, own_second, first, second, own_coefs, near_coefs, ys):
    return pl.pallas_call(
        near_kernel,
        out_shape=tuple(level_shape(layers, ys) for layers in (8, *NEAR_LAYERS)),
        in_specs=specs("svvvvvv"),
        out_specs=tuple(specs("vvvv")),
        compiler_params=params(8),
        cost_estimate=cost(0, 0),
    )(counts, own_first, own_second, first, second, own_coefs, near_coefs)


def first_steps(counts, first, own_coefs, levels, shape, rows):
    ys, zs = shape[1], shape[2]
    return pl.pallas_call(
        first_kernel,
        out_shape=(
            jax.ShapeDtypeStruct((2, *shape[1:]), jnp.bfloat16),
            factors(3, ys, zs),
            *[level_shape(2, ys)] * 4,
        ),
        in_specs=specs("svvvvvv"),
        out_specs=tuple(specs("vvvvvv")),
        scratch_shapes=[pltpu.VMEM((rows, zs), jnp.float32), pltpu.VMEM((128, zs), jnp.float32)],
        compiler_params=params(8),
        cost_estimate=cost(0, 0),
    )(counts, first, own_coefs, *levels)


def second_steps(counts, second, done, own_coefs, far_coefs, levels, shape):
    ys = shape[1]
    return pl.pallas_call(
        second_kernel,
        out_shape=jax.ShapeDtypeStruct(shape, jnp.bfloat16),
        in_specs=specs("svvvvvvvv"),
        out_specs=specs("v")[0],
        scratch_shapes=[pltpu.VMEM((2, ys, 2, ROWS, HALF), jnp.float32)] * 4,
        compiler_params=params(8),
        cost_estimate=cost(0, 0),
    )(counts, second, done, own_coefs, far_coefs, *levels)


def products(ahead, state, order_next, order_here):
    return pl.pallas_call(
        product_kernel,
        out_shape=jax.ShapeDtypeStruct((K, K), jnp.bfloat16),
        in_specs=specs("vvvv"),
        out_specs=specs("v")[0],
        compiler_params=params(16),
        cost_estimate=cost(0, 0),
    )(ahead, state, order_next, order_here)


def save(state):
    return pl.pallas_call(
        save_kernel,
        out_shape=jax.ShapeDtypeStruct(state.shape, state.dtype),
        in_specs=specs("v"),
        out_specs=specs("a")[0],
        scratch_shapes=[pltpu.SemaphoreType.DMA],
        compiler_params=params(4),
        cost_estimate=cost(0, 2 * state.size * state.dtype.itemsize),
    )(state)


def mixed_swap(value, along, across, core_along):
    total, slabs = lax.axis_size("seg"), lax.axis_size("space")
    route = []
    for s in range(total):
        for x in range(slabs):
            if core_along:
                to = (s ^ along, x) if x % 2 else (s, x ^ across)
            else:
                to = (s ^ along, x ^ across)
            route.append((s * slabs + x, to[0] * slabs + to[1]))
    return lax.ppermute(value, ("seg", "space"), route)


def per_device(basis, diffusivity, velocity, step_counts, block_order):
    start = basis[0]
    total = lax.axis_size("seg")
    slabs = lax.axis_size("space")
    cells = start.shape[0] * slabs * start.shape[1] * start.shape[2]

    ahead = lax.ppermute(start, "seg", [((i + 1) % total, i) for i in range(total)])
    ys, zs = start.shape[1], start.shape[2]
    planes = start.reshape(-1, BLOCK, K)
    first, second, fields = pack(planes, diffusivity[0].transpose(1, 0, 2), velocity[0].transpose(0, 2, 1, 3))
    near_first = exchange_pairs(first, "space", 0)
    near_second = exchange_pairs(second, "space", 0)
    far_first = exchange_pairs(first, "space", 1)
    far_second = exchange_pairs(second, "space", 1)
    own_coefs, near_coefs, order_here, order_next = spread(fields, near_first, block_order, ys)
    levels = near_steps(step_counts, first, second, near_first, near_second, own_coefs, near_coefs, ys)
    image_first, far_coefs, *levels = first_steps(
        step_counts, far_first, own_coefs, levels, start.shape, fields.shape[0]
    )
    state = second_steps(step_counts, far_second, image_first, own_coefs, far_coefs, levels, start.shape)
    raw = products(ahead, state, order_next, order_here)

    bit = 1
    while 2 * bit < slabs:
        raw = to_bf16(to_f32(raw) + to_f32(swap(raw, "space", bit)))
        bit *= 2
    odd = lax.axis_index("space") % 2 == 1
    upper = lax.axis_index("seg") % 2 == 1

    def my_half(full):
        return jnp.where(odd, full[:, HALF:], full[:, :HALF])

    def my_rows(full):
        return jnp.where(odd, full[HALF:], full[:HALF])

    def folded(rows):
        return jnp.concatenate([rows[:, :HALF], rows[:, HALF:]], 0)

    def unfolded(part):
        return jnp.concatenate([part[:HALF], part[HALF:]], 1)

    def both_halves(part):
        rest = swap(part, "space", 1)
        return jnp.where(odd, jnp.concatenate([rest, part], 1), jnp.concatenate([part, rest], 1))

    def both_parts(part):
        rest = swap(part, "space", 1)
        low = jnp.where(odd, rest, part)
        high = jnp.where(odd, part, rest)
        rows = jnp.concatenate([unfolded(low), unfolded(high)], 0)
        return jnp.where(upper, jnp.concatenate([low, high], 1), rows)

    def chained(later, earlier):
        return to_f32(later) + to_f32(earlier) + mul(later, earlier)

    scale = coupling / math.sqrt(K * cells)

    def factor(one, two):
        return to_bf16((to_f32(one) + to_f32(two)) * scale)

    straight = mixed_swap(raw, 1, bit, True)
    diagonal = mixed_swap(jnp.where(upper, folded(my_rows(raw)), my_half(raw)), 1, bit, False)
    straight_other = swap(straight, "space", 1)
    across = jnp.where(odd, straight_other, straight)
    along = jnp.where(odd, straight, straight_other)
    mine = factor(raw, across)
    columns = factor(my_half(along), diagonal)
    rows = factor(my_rows(along), unfolded(diagonal))
    up = to_f32(my_half(mine)) + to_f32(columns) + mul(mine, columns)
    down = to_f32(my_rows(mine)) + to_f32(rows) + mul(rows, mine)
    half = jnp.where(upper, to_bf16(up), folded(to_bf16(down)))
    got_part = swap(half, "seg", 2) if total > 2 else None

    state, diagonal, half = lax.optimization_barrier((state, diagonal, half))
    image = save(state)
    theirs = factor(along, both_parts(diagonal))
    block = chained(jnp.where(upper, mine, theirs), jnp.where(upper, theirs, mine))
    wide = jnp.where(upper, block, to_f32(mine))
    bit = 2
    while bit < total:
        higher = (lax.axis_index("seg") // bit) % 2 == 1
        block = to_bf16(block)
        got = both_parts(got_part) if bit == 2 else both_halves(swap(my_half(block), "seg", bit))
        wide = jnp.where(higher, wide + to_f32(got) + mul(to_bf16(wide), got), wide)
        if 2 * bit < total:
            block = chained(jnp.where(higher, block, got), jnp.where(higher, got, block))
        bit *= 2
    monodromy = wide + jnp.eye(K, dtype=jnp.float32)
    return (image[None], monodromy[None])


def solution(mesh):
    in_specs = (
        P(("groups", "seg"), "space", None, None, None),
        P(("groups", "seg"), "space", None, None),
        P(("groups", "seg"), None, "space", None, None),
        P(("groups", "seg")),
        P("groups", None),
    )
    out_specs = (P(("groups", "seg"), "space", None, None, None), P(("groups", "seg"), None, None))
    return jax.shard_map(
        per_device, mesh=mesh, in_specs=in_specs, out_specs=out_specs, check_vma=False
    )
```
